32 devices in a mesh: grp: 2 (over x), blk: 8 (over z, y), proj: 2 (over core).
Axes of the slice: x: 2, y: 2, z: 4, core: 2. Of those that a mesh axis runs over, the one named last changes fastest.
Arguments:
- doc_inputs: bfloat16 [8192, 2, 64, 128], P(('grp', 'blk'), 'proj'), parts along dimension 0, may hold values from -6 to 6
- doc_outgrads: bfloat16 [8192, 2, 64, 128], P(('grp', 'blk'), 'proj'), parts along dimension 0, may hold values from -6 to 6
- token_mask: int32 [8192, 128], P(('grp', 'blk')), parts along dimension 0, may hold values 0 or 1
- query_grads: bfloat16 [4096, 8192], P(('grp', 'blk'), 'proj'), parts along dimension 0, may hold values from -0.0078125 to 0.0078125
Outputs:
- scores: float32 [8192, 2048], P(('grp', 'blk', 'proj')), parts along dimension 0
The draws below stay inside these ranges and needn't reach their ends.
There are 2 independent parts, one for each index of `grp`. The reference program is written for one: setup_inputs(seed, part) draws one part's arguments, and reference() takes and returns one part's arrays. A program takes and returns all parts, laid end to end along the dimension named above; each array names one. Nothing has to cross between parts.
All inputs are finite; a program needn't handle non-finite values. No bound on the sum of `token_mask` on one device may be relied on, other than what follows from the above.
Results may differ from the reference program's by a relative error of at most 0.0029.
Values may be sent and summed in bfloat16 or wider, within the bound.
No kernel may reach another device: no remote copies, remote signals or barrier semaphores. Data moves between devices by JAX's collectives and lax.ppermute only.
A program may use at most 128 MiB of HBM per device.

```python
import jax
import jax.numpy as jnp

RANK = 64
LAYERS = 2
TOKLEN = 128
DOCS = 4096
QUERIES = 2048


def touch_ends(drawn, rng, least, largest):
    longest = drawn.shape.index(max(drawn.shape))
    spots = []
    for shift in (0, 1):
        where = [jax.random.randint(jax.random.fold_in(rng, axis), (), 0, length) for axis, length in enumerate(drawn.shape)]
        where[longest] = (where[longest] + shift) % drawn.shape[longest]
        spots.append(tuple(where))
    return drawn.at[spots[0]].set(least).at[spots[1]].set(largest)


def shard_levels(rng, extent, shards, low, top_value):
    def one(position, blocks):
        steps = jax.random.uniform(jax.random.fold_in(jax.random.fold_in(rng, 6), position), (blocks,), jnp.float32, low / len(shards), top_value / len(shards))
        return jnp.repeat(jnp.exp(steps), extent[position] // blocks).reshape((-1,) + (1,) * (len(extent) - position - 1))

    factor_of = one(*shards[0])
    for cut in shards[1:]:
        factor_of = factor_of * one(*cut)
    return factor_of


def noise(stream_key, dims, width, bound, split=(), kind=jnp.bfloat16):
    entries = width * jax.random.normal(stream_key, dims, jnp.float32)
    if split:
        entries = entries * shard_levels(stream_key, dims, split, -0.22, 0.18)
    return jnp.clip(entries, -bound, bound).astype(kind)


def setup_inputs(seed: int = 0, part: int = 0) -> dict:
    streams_of = jax.random.split(jax.random.key(seed), 5)
    part_keys = jax.random.split(jax.random.fold_in(streams_of[4], part), 5)
    return {
        "doc_inputs": noise(part_keys[0], (DOCS, LAYERS, RANK, TOKLEN), 1.0, 6.0, ((0, 8), (1, 2))),
        "doc_outgrads": noise(part_keys[1], (DOCS, LAYERS, RANK, TOKLEN), 1.0, 6.0, ((0, 8), (1, 2))),
        "token_mask": touch_ends((jax.random.randint(part_keys[2], (DOCS, TOKLEN), 0, 2) < 1).astype(jnp.int32), jax.random.fold_in(part_keys[2], 1), 0, 1),
        "query_grads": noise(part_keys[3], (QUERIES, LAYERS * RANK * RANK), (LAYERS * RANK * RANK * TOKLEN // 2) ** -0.5, 0.0078125, ((0, 8), (1, 2))),
    }


def reference(doc_inputs, doc_outgrads, token_mask, query_grads):
    masked = doc_outgrads * token_mask[:, None, None, :].astype(jnp.bfloat16)
    doc_grads = jnp.einsum("dlit,dljt->dlij", doc_inputs.astype(jnp.float32), masked.astype(jnp.float32)).astype(jnp.bfloat16)
    doc_flat = doc_grads.reshape(DOCS, LAYERS * RANK * RANK)
    return jnp.dot(doc_flat, query_grads.T, preferred_element_type=jnp.float32)
```

```python
import jax
import jax.numpy as jnp
from jax import lax
from jax.sharding import PartitionSpec as P


def on_device(doc_inputs, doc_outgrads, token_mask, query_grads):
    blk = lax.axis_size("blk")
    places = blk // 2
    me = lax.axis_index("blk")
    place, side = me // 2, me % 2
    core = lax.axis_index("proj")
    docs = doc_inputs.shape[0]
    rank = doc_inputs.shape[2]
    queries = query_grads.shape[0]
    half = query_grads.shape[1] // 2
    part = docs // 2

    across = [(b, b ^ 1) for b in range(blk)]
    onward = [(b, (b + 2) % blk) for b in range(blk)]
    cores = [(0, 1), (1, 0)]
    diagonal = [(2 * b + c, 2 * (b ^ 1) + (c ^ 1)) for b in range(blk) for c in range(2)]

    def columns(array, which):
        return lax.dynamic_slice_in_dim(array, which * half, half, 1)

    mine = columns(query_grads, side)
    other = lax.ppermute(columns(query_grads, 1 - side), "blk", across)

    masked = doc_outgrads * token_mask[:, None, None, :].astype(jnp.bfloat16)
    formed = jnp.einsum(
        "dlit,dljt->dlij", doc_inputs, masked, preferred_element_type=jnp.float32
    ).astype(jnp.bfloat16)
    flat = formed.reshape(docs, rank * rank)
    flat = jnp.where(core == 0, flat, jnp.roll(flat, part, 0))
    kept = columns(flat, side)
    received = lax.ppermute(columns(flat, 1 - side), "blk", across)
    rows = jnp.concatenate([kept, received], 0)

    out = jnp.zeros((part, blk * queries), jnp.float32)
    contract = (((1,), (1,)), ((), ()))
    flows = [mine, other]
    for step in range(places):
        origin = (place - step + places) % places
        following = []
        if step + 1 < places:
            following = [lax.ppermute(block, "blk", onward) for block in flows]
        partials = [
            lax.dot_general(rows, block, contract, preferred_element_type=jnp.float32)
            for block in flows
        ]
        for which in range(2):
            near, far = partials[which], partials[1 - which]
            total = near[:part]
            total += lax.ppermute(near[part:2 * part].astype(jnp.bfloat16), "proj", cores).astype(jnp.float32)
            total += lax.ppermute(far[2 * part:3 * part].astype(jnp.bfloat16), "blk", across).astype(jnp.float32)
            total += lax.ppermute(far[3 * part:].astype(jnp.bfloat16), ("blk", "proj"), diagonal).astype(jnp.float32)
            owner = origin * 2 + (side if which == 0 else 1 - side)
            out = lax.dynamic_update_slice_in_dim(out, total, owner * queries, 1)
        flows = following
    return out


def solution(mesh):
    placed = (
        P(("grp", "blk"), "proj", None, None),
        P(("grp", "blk"), "proj", None, None),
        P(("grp", "blk"), None),
        P(("grp", "blk"), "proj"),
    )
    return jax.shard_map(
        on_device,
        mesh=mesh,
        in_specs=placed,
        out_specs=P(("grp", "blk", "proj"), None),
        check_vma=False,
    )
```

```python
import functools

import jax
import jax.numpy as jnp
from jax import lax
from jax.experimental import pallas as pl
from jax.experimental.pallas import tpu as pltpu
from jax.sharding import PartitionSpec as P

LANES = 128
VMEM_LIMIT = 48 * 1024 * 1024
ANYWHERE = pl.BlockSpec(memory_space=pl.ANY)
NT = (((1,), (1,)), ((), ()))


def form_body(rows, rank, spot, inputs, outgrads, mask, _after, kept, sent, rounds):
    def one(d, carry):
        masked = outgrads[d] * mask[pl.ds(d, 1), :].astype(jnp.bfloat16)
        twice = jnp.concatenate([masked, masked], 0)
        product = lax.dot_general(inputs[d], twice, NT, preferred_element_type=jnp.float32)
        rounds[pl.ds(d, rank, stride=rows), :] = product
        return carry

    lax.fori_loop(0, rows, one, 0, unroll=8)
    first = lax.broadcasted_iota(jnp.int32, (rows, LANES), 1) < rank
    for out, side in ((kept, spot[0]), (sent, 1 - spot[0])):
        for k in range(rank // 4):
            at = pl.multiple_of((side * (rank // 2) + 2 * k) * rows, rows)
            even = rounds[pl.ds(at, rows), :]
            odd = rounds[pl.ds(at + rows, rows), :]
            out[:, k * LANES:(k + 1) * LANES] = jnp.where(first, even, odd).astype(jnp.bfloat16)


def form(doc_inputs, doc_outgrads, token_mask, side, core, after):
    docs, rank, length = doc_inputs.shape
    rows = 32
    steps = docs // rows
    half = rank * rank // 2

    def at(g, spot):
        return lax.rem(g + spot[1] * (steps // 2), steps)

    return pl.pallas_call(
        functools.partial(form_body, rows, rank),
        grid_spec=pltpu.PrefetchScalarGridSpec(
            num_scalar_prefetch=1,
            grid=(steps,),
            in_specs=[
                pl.BlockSpec((rows, rank, length), lambda g, spot: (at(g, spot), 0, 0)),
                pl.BlockSpec((rows, rank, length), lambda g, spot: (at(g, spot), 0, 0)),
                pl.BlockSpec((rows, length), lambda g, spot: (at(g, spot), 0)),
                ANYWHERE,
            ],
            out_specs=[pl.BlockSpec((rows, half), lambda g, spot: (g, 0))] * 2,
            scratch_shapes=[pltpu.VMEM((rank * rows, LANES), jnp.float32)],
        ),
        out_shape=[jax.ShapeDtypeStruct((docs, half), jnp.bfloat16)] * 2,
        compiler_params=pltpu.CompilerParams(vmem_limit_bytes=VMEM_LIMIT),
        cost_estimate=pl.CostEstimate(
            flops=2 * docs * rank * rank * length, bytes_accessed=4 * docs * rank * length + 2 * docs * rank * rank, transcendentals=0
        ),
    )(jnp.stack([side, core]).astype(jnp.int32), doc_inputs, doc_outgrads, token_mask, after)


def score_body(own, far, block, _after, near, mate, across, diagonal):
    part = near.shape[0]

    def dot(rows):
        return lax.dot_general(rows, block[...], NT, preferred_element_type=jnp.float32)

    near[...] = dot(own[:part, :])
    mate[...] = dot(own[part:, :]).astype(jnp.bfloat16)
    across[...] = dot(far[:part, :]).astype(jnp.bfloat16)
    diagonal[...] = dot(far[part:, :]).astype(jnp.bfloat16)


def score(own, far, block, after):
    docs, depth = own.shape
    queries = block.shape[0]
    shape = (docs // 2, queries)
    whole = pl.BlockSpec(memory_space=pltpu.VMEM)
    return pl.pallas_call(
        score_body,
        in_specs=[whole, whole, whole, ANYWHERE],
        out_specs=[whole] * 4,
        out_shape=[jax.ShapeDtypeStruct(shape, jnp.float32)] + [jax.ShapeDtypeStruct(shape, jnp.bfloat16)] * 3,
        compiler_params=pltpu.CompilerParams(vmem_limit_bytes=VMEM_LIMIT),
        cost_estimate=pl.CostEstimate(
            flops=4 * docs * queries * depth, bytes_accessed=4 * docs * depth + 2 * queries * depth, transcendentals=0
        ),
    )(own, far, block, after)


def on_device(doc_inputs, doc_outgrads, token_mask, query_grads):
    blk = lax.axis_size("blk")
    places = blk // 2
    me = lax.axis_index("blk")
    place, side = me // 2, me % 2
    core = lax.axis_index("proj")
    docs = doc_inputs.shape[0]
    queries = query_grads.shape[0]
    half = query_grads.shape[1] // 2
    part = docs // 2

    across = [(b, b ^ 1) for b in range(blk)]
    onward = [(b, (b + 2) % blk) for b in range(blk)]
    cores = [(0, 1), (1, 0)]
    diagonal = [(2 * b + c, 2 * (b ^ 1) + (c ^ 1)) for b in range(blk) for c in range(2)]

    def columns(array, which):
        return lax.dynamic_slice_in_dim(array, which * half, half, 1)

    flows = [[columns(query_grads, side)], [lax.ppermute(columns(query_grads, 1 - side), "blk", across)]]
    for step in range(1, places):
        for flow in flows:
            flow.append(lax.ppermute(flow[-1], "blk", onward))

    own, sent = form(
        doc_inputs.reshape(docs, *doc_inputs.shape[2:]), doc_outgrads.reshape(docs, *doc_outgrads.shape[2:]),
        token_mask, side, core, flows[0][min(1, places - 1)],
    )
    far = lax.ppermute(sent, "blk", across)

    out = jnp.zeros((part, blk * queries), jnp.float32)
    last = token_mask
    for step in range(places):
        origin = (place - step + places) % places
        pieces = []
        for flow in flows:
            pieces.append(score(own, far, flow[step], last))
            last = pieces[-1][0]
        for which in range(2):
            near, mate = pieces[which][:2]
            beside, opposite = pieces[1 - which][2:]
            total = near + lax.ppermute(mate, "proj", cores).astype(jnp.float32)
            total += lax.ppermute(beside, "blk", across).astype(jnp.float32)
            total += lax.ppermute(opposite, ("blk", "proj"), diagonal).astype(jnp.float32)
            owner = origin * 2 + (side if which == 0 else 1 - side)
            out = lax.dynamic_update_slice_in_dim(out, total, owner * queries, 1)
    return out


def solution(mesh):
    placed = (
        P(("grp", "blk"), "proj", None, None),
        P(("grp", "blk"), "proj", None, None),
        P(("grp", "blk"), None),
        P(("grp", "blk"), "proj"),
    )
    return jax.shard_map(
        on_device,
        mesh=mesh,
        in_specs=placed,
        out_specs=P(("grp", "blk", "proj"), None),
        check_vma=False,
    )
```

```python
import functools

import jax
import jax.numpy as jnp
from jax import lax
from jax.experimental import pallas as pl
from jax.experimental.pallas import tpu as pltpu
from jax.sharding import PartitionSpec as P

LANES = 128
VMEM_LIMIT = 48 * 1024 * 1024
ANYWHERE = pl.BlockSpec(memory_space=pl.ANY)
SCALARS = pl.BlockSpec(memory_space=pltpu.SMEM)
WHOLE = pl.BlockSpec(memory_space=pltpu.VMEM)
NT = (((1,), (1,)), ((), ()))
bf16, f32 = jnp.bfloat16, jnp.float32


def prepare_body(spot, query_grads, mine, other):
    rank = LANES // 2
    width = query_grads.shape[1]
    for out, side in ((mine, spot[0]), (other, 1 - spot[0])):
        for m in range(width // 4 // LANES):
            at = pl.multiple_of(side * (width // 4) + m * LANES, LANES)
            low = query_grads[:, pl.ds(at, LANES)]
            high = query_grads[:, pl.ds(at + width // 2, LANES)]
            out[:, 2 * m * LANES:(2 * m + 1) * LANES] = jnp.concatenate([low[:, :rank], high[:, :rank]], 1)
            out[:, (2 * m + 1) * LANES:(2 * m + 2) * LANES] = jnp.concatenate([low[:, rank:], high[:, rank:]], 1)


def prepare(query_grads, spot):
    rows, width = query_grads.shape
    return pl.pallas_call(
        prepare_body,
        in_specs=[SCALARS, WHOLE],
        out_specs=[WHOLE] * 2,
        out_shape=[jax.ShapeDtypeStruct((rows, width // 2), bf16)] * 2,
        compiler_params=pltpu.CompilerParams(vmem_limit_bytes=VMEM_LIMIT),
    )(spot, query_grads)


def form_body(rows, rank, spot, inputs, outgrads, mask, _after, _later, kept, sent, rounds):
    def one(d, carry):
        masked = outgrads[d] * mask[pl.ds(d, 1), :].astype(bf16)
        product = lax.dot_general(inputs[d], masked, NT, preferred_element_type=f32)
        pairs = jnp.concatenate([product[:rank // 2], product[rank // 2:]], 1)
        rounds[pl.ds(d, rank // 2, stride=rows), :] = pairs
        return carry

    lax.fori_loop(0, rows, one, 0, unroll=8)
    for out, side in ((kept, spot[0]), (sent, 1 - spot[0])):
        for k in range(rank // 4):
            at = pl.multiple_of((side * (rank // 4) + k) * rows, rows)
            out[:, k * LANES:(k + 1) * LANES] = rounds[pl.ds(at, rows), :].astype(bf16)


def form(doc_inputs, doc_outgrads, token_mask, spot, after, later):
    docs, rank, length = doc_inputs.shape
    rows = 32
    steps = docs // rows
    half = rank * rank // 2

    def at(g, spot):
        return lax.rem(g + spot[1] * (steps // 2), steps)

    return pl.pallas_call(
        functools.partial(form_body, rows, rank),
        grid_spec=pltpu.PrefetchScalarGridSpec(
            num_scalar_prefetch=1,
            grid=(steps,),
            in_specs=[
                pl.BlockSpec((rows, rank, length), lambda g, spot: (at(g, spot), 0, 0)),
                pl.BlockSpec((rows, rank, length), lambda g, spot: (at(g, spot), 0, 0)),
                pl.BlockSpec((rows, length), lambda g, spot: (at(g, spot), 0)),
                ANYWHERE,
                ANYWHERE,
            ],
            out_specs=[pl.BlockSpec((rows, half), lambda g, spot: (g, 0))] * 2,
            scratch_shapes=[pltpu.VMEM((rank // 2 * rows, LANES), f32)],
        ),
        out_shape=[jax.ShapeDtypeStruct((docs, half), bf16)] * 2,
        compiler_params=pltpu.CompilerParams(vmem_limit_bytes=VMEM_LIMIT),
        cost_estimate=pl.CostEstimate(
            flops=40 * docs * rank * rank * length, bytes_accessed=4 * docs * rank * length + 2 * docs * rank * rank, transcendentals=0
        ),
    )(spot, doc_inputs, doc_outgrads, token_mask, after, later)


def tie_body(array, _after, out):
    pass


def tie(array, after):
    return pl.pallas_call(
        tie_body,
        in_specs=[ANYWHERE] * 2,
        out_specs=ANYWHERE,
        out_shape=jax.ShapeDtypeStruct(array.shape, array.dtype),
        input_output_aliases={0: 0},
        compiler_params=pltpu.CompilerParams(vmem_limit_bytes=VMEM_LIMIT),
    )(array, after)


def score_body(spot, own, far, first, second, _after, _later, keep, give):
    part = own.shape[0] // 2
    queries = first.shape[0]
    for block, slot in ((first, spot[0]), (second, 1 - spot[0])):
        at = pl.ds(pl.multiple_of(slot * queries, queries), queries)

        def dot(rows):
            return lax.dot_general(rows, block[...], NT, preferred_element_type=f32)

        keep[:part, at] = dot(own[:part, :])
        keep[part:, at] = dot(far[:part, :])
        give[:part, at] = dot(own[part:, :]).astype(bf16)
        give[part:, at] = dot(far[part:, :]).astype(bf16)


def score(spot, own, far, first, second, after, later):
    docs, depth = own.shape
    queries = first.shape[0]
    return pl.pallas_call(
        score_body,
        in_specs=[SCALARS, WHOLE, WHOLE, WHOLE, WHOLE, ANYWHERE, ANYWHERE],
        out_specs=[WHOLE] * 2,
        out_shape=[jax.ShapeDtypeStruct((docs, 2 * queries), f32), jax.ShapeDtypeStruct((docs, 2 * queries), bf16)],
        compiler_params=pltpu.CompilerParams(vmem_limit_bytes=VMEM_LIMIT),
        cost_estimate=pl.CostEstimate(
            flops=docs * queries, bytes_accessed=docs * queries, transcendentals=0
        ),
    )(spot, own, far, first, second, after, later)


def on_device(doc_inputs, doc_outgrads, token_mask, query_grads):
    blk = lax.axis_size("blk")
    places = blk // 2
    me = lax.axis_index("blk")
    place, side = me // 2, me % 2
    spot = jnp.stack([side, lax.axis_index("proj")]).astype(jnp.int32)
    docs = doc_inputs.shape[0]
    queries = query_grads.shape[0]
    part = docs // 2

    across = [(b, b ^ 1) for b in range(blk)]
    onward = [(b, (b + 2) % blk) for b in range(blk)]
    cores = [(0, 1), (1, 0)]

    mine, other = prepare(query_grads, spot)
    flows = [[mine], [lax.ppermute(other, "blk", across)]]
    for step in range(1, places):
        for flow in flows:
            flow.append(lax.ppermute(flow[-1], "blk", onward))

    own, sent = form(
        doc_inputs.reshape(docs, *doc_inputs.shape[2:]), doc_outgrads.reshape(docs, *doc_outgrads.shape[2:]),
        token_mask, spot, flows[0][min(1, places - 1)], flows[1][0],
    )
    far = lax.ppermute(tie(sent, flows[0][min(2, places - 1)]), "blk", across)

    out = jnp.zeros((part, blk * queries), f32)
    last = [flows[1][min(1, places - 1)], token_mask, token_mask]
    for step in range(places):
        origin = (place - step + places) % places
        keep, give = score(spot, own, far, flows[0][step], flows[1][step], last[0], last[1 + step])
        last[0] = give
        got = lax.ppermute(give, "proj", cores).astype(f32)
        beside = lax.ppermute((keep[part:] + got[part:]).astype(bf16), "blk", across)
        last.append(beside)
        out = lax.dynamic_update_slice_in_dim(out, keep[:part] + got[:part] + beside.astype(f32), origin * (2 * queries), 1)
    return out


def solution(mesh):
    placed = (
        P(("grp", "blk"), "proj", None, None),
        P(("grp", "blk"), "proj", None, None),
        P(("grp", "blk"), None),
        P(("grp", "blk"), "proj"),
    )
    return jax.shard_map(
        on_device,
        mesh=mesh,
        in_specs=placed,
        out_specs=P(("grp", "blk", "proj"), None),
        check_vma=False,
    )
```

```python
import functools

import jax
import jax.numpy as jnp
from jax import lax
from jax.experimental import pallas as pl
from jax.experimental.pallas import tpu as pltpu
from jax.sharding import PartitionSpec as P

LANES = 128
VMEM_LIMIT = 48 * 1024 * 1024
ANYWHERE = pl.BlockSpec(memory_space=pl.ANY)
SCALARS = pl.BlockSpec(memory_space=pltpu.SMEM)
WHOLE = pl.BlockSpec(memory_space=pltpu.VMEM)
NT = (((1,), (1,)), ((), ()))
bf16, f32 = jnp.bfloat16, jnp.float32
LIMIT = pltpu.CompilerParams(vmem_limit_bytes=VMEM_LIMIT)


def shaped(kind, *shape):
    return jax.ShapeDtypeStruct(shape, kind)


def prepare_body(spot, query_grads, mine, start, other):
    rank = LANES // 2
    width = query_grads.shape[1]
    for outs, side in (((mine, start), spot[0]), ((other,), 1 - spot[0])):
        for m in range(width // 4 // LANES):
            at = pl.multiple_of(side * (width // 4) + m * LANES, LANES)
            low = query_grads[:, pl.ds(at, LANES)]
            high = query_grads[:, pl.ds(at + width // 2, LANES)]
            for odd, block in enumerate((
                jnp.concatenate([low[:, :rank], high[:, :rank]], 1),
                jnp.concatenate([low[:, rank:], high[:, rank:]], 1),
            )):
                k = 2 * m + odd
                for out in outs:
                    if k * LANES < out.shape[1]:
                        out[:, k * LANES:(k + 1) * LANES] = block


def prepare(query_grads, spot, stay):
    rows, width = query_grads.shape
    return pl.pallas_call(
        prepare_body,
        in_specs=[SCALARS, WHOLE],
        out_specs=[WHOLE] * 3,
        out_shape=[shaped(bf16, rows, width // 2), shaped(bf16, rows, stay), shaped(bf16, rows, width // 2)],
        compiler_params=LIMIT,
    )(spot, query_grads)


def form_body(rows, rank, spot, inputs, outgrads, mask, *refs):
    kept, lent, sent, sent_lent, rounds = refs[-5:]
    for d in range(rows):
        masked = outgrads[d] * mask[d:d + 1, :].astype(bf16)
        product = lax.dot_general(inputs[d], masked, NT, preferred_element_type=f32)
        pairs = jnp.concatenate([product[:rank // 2], product[rank // 2:]], 1)
        rounds[pl.ds(d, rank // 2, stride=rows), :] = pairs
    stay = sent.shape[1] // LANES
    for which in range(2):
        side = spot[0] if which == 0 else 1 - spot[0]
        for k in range(rank // 4):
            at = pl.multiple_of((side * (rank // 4) + k) * rows, rows)
            block = rounds[pl.ds(at, rows), :].astype(bf16)
            if which == 0:
                kept[:, k * LANES:(k + 1) * LANES] = block
                if k >= stay:
                    lent[:, (k - stay) * LANES:(k - stay + 1) * LANES] = block
            elif k < stay:
                sent[:, k * LANES:(k + 1) * LANES] = block
            else:
                sent_lent[:, (k - stay) * LANES:(k - stay + 1) * LANES] = block


def form(doc_inputs, doc_outgrads, token_mask, spot, stay, *after):
    docs, rank, length = doc_inputs.shape
    rows = 64
    steps = docs // rows
    half = rank * rank // 2
    widths = (half, half - stay, stay, half - stay)

    def at(g, spot):
        return lax.rem(g + spot[1] * (steps // 2), steps)

    return pl.pallas_call(
        functools.partial(form_body, rows, rank),
        grid_spec=pltpu.PrefetchScalarGridSpec(
            num_scalar_prefetch=1,
            grid=(steps,),
            in_specs=[
                pl.BlockSpec((rows, rank, length), lambda g, spot: (at(g, spot), 0, 0)),
                pl.BlockSpec((rows, rank, length), lambda g, spot: (at(g, spot), 0, 0)),
                pl.BlockSpec((rows, length), lambda g, spot: (at(g, spot), 0)),
            ] + [ANYWHERE] * len(after),
            out_specs=[pl.BlockSpec((rows, width), lambda g, spot: (g, 0)) for width in widths],
            scratch_shapes=[pltpu.VMEM((rank // 2 * rows, LANES), f32)],
        ),
        out_shape=[shaped(bf16, docs, width) for width in widths],
        compiler_params=LIMIT,
        cost_estimate=pl.CostEstimate(
            flops=40 * docs * rank * rank * length, bytes_accessed=4 * docs * rank * length + 2 * docs * rank * rank, transcendentals=0
        ),
    )(spot, doc_inputs, doc_outgrads, token_mask, *after)


def tie(arrays, *after):
    count = len(arrays)
    return pl.pallas_call(
        lambda *refs: None,
        in_specs=[ANYWHERE] * (count + len(after)),
        out_specs=[ANYWHERE] * count,
        out_shape=[shaped(a.dtype, *a.shape) for a in arrays],
        input_output_aliases={i: i for i in range(count)},
        compiler_params=LIMIT,
    )(*arrays, *after)


def store_products(spot, blocks, rows_of, keep, give):
    part = keep.shape[0] // 2
    queries = blocks[0].shape[0]
    for block, slot in zip(blocks, (spot[0], 1 - spot[0])):
        at = pl.ds(pl.multiple_of(slot * queries, queries), queries)
        products = rows_of(block)
        keep[:part, at] = products[0]
        give[:part, at] = products[1].astype(bf16)
        keep[part:, at] = products[2]
        give[part:, at] = products[3].astype(bf16)


def dot(rows, block):
    return lax.dot_general(rows, block, NT, preferred_element_type=f32)


def own_body(stay, spot, own, far, far_lent, first, second, first_stay, second_stay, *refs):
    keep, give = refs[-2:]
    part = own.shape[0] // 2

    def all_features(block):
        out = []
        for h in range(2):
            out.append(dot(own[h * part:(h + 1) * part, :], block[...]))
        for h in range(2):
            rows = slice(h * part, (h + 1) * part)
            out.append(dot(far[rows, :], block[:, :stay]) + dot(far_lent[rows, :], block[:, stay:]))
        return out

    def staying(block):
        out = []
        for h in range(2):
            out.append(dot(own[h * part:(h + 1) * part, :stay], block[:, :stay]))
        for h in range(2):
            out.append(dot(far[h * part:(h + 1) * part, :], block[:, :stay]))
        return out

    @pl.when(spot[2] == 1)
    def _():
        store_products(spot, (first, second), all_features, keep, give)

    @pl.when(spot[2] == 0)
    def _():
        store_products(spot, (first_stay, second_stay), staying, keep, give)


def lent_body(stay, spot, near, far, first, second, *refs):
    keep, give = refs[-2:]
    part = near.shape[0] // 2

    def products(block):
        return [
            dot(rows[h * part:(h + 1) * part, :], block[:, stay:]) for rows in (near, far) for h in range(2)
        ]

    @pl.when(spot[2] == 1)
    def _():
        store_products(spot, (first, second), products, keep, give)


def score(body, stay, spot, operands, docs, queries, after):
    return pl.pallas_call(
        functools.partial(body, stay),
        in_specs=[SCALARS] + [WHOLE] * len(operands) + [ANYWHERE] * len(after),
        out_specs=[WHOLE] * 2,
        out_shape=[shaped(f32, docs, 2 * queries), shaped(bf16, docs, 2 * queries)],
        compiler_params=LIMIT,
        cost_estimate=pl.CostEstimate(flops=docs * queries, bytes_accessed=docs * queries, transcendentals=0),
    )(spot, *operands, *after)


def on_device(doc_inputs, doc_outgrads, token_mask, query_grads):
    blk = lax.axis_size("blk")
    places = blk // 2
    me = lax.axis_index("blk")
    place, side = me // 2, me % 2
    docs, rank = doc_inputs.shape[0], doc_inputs.shape[2]
    queries = query_grads.shape[0]
    part = docs // 2
    half = rank * rank // 2
    doc_inputs = doc_inputs.reshape(docs, *doc_inputs.shape[2:])
    doc_outgrads = doc_outgrads.reshape(docs, *doc_outgrads.shape[2:])
    lending = places == 4
    stay = half * 10 // 16
    inner = jnp.where((place == 1) | (place == 2), 1, 0) if lending else 1
    spot = jnp.stack([side, lax.axis_index("proj"), inner]).astype(jnp.int32)

    across = [(b, b ^ 1) for b in range(blk)]
    onward = [(b, (b + 2) % blk) for b in range(blk)]
    cores = [(0, 1), (1, 0)]

    mine, mine_stay, sending = prepare(query_grads, spot, stay)
    other = lax.ppermute(sending, "blk", across)

    def take(keep, give, far_across, far_cores):
        got = far_cores(give)
        beside = far_across((keep[part:] + got[part:].astype(f32)).astype(bf16))
        return keep[:part] + got[:part].astype(f32) + beside.astype(f32), beside

    def swap_across(x):
        return lax.ppermute(x, "blk", across)

    def swap_cores(x):
        return lax.ppermute(x, "proj", cores)

    out = jnp.zeros((part, blk * queries), f32)
    if not lending:
        flows = [[mine], [other]]
        for step in range(1, places):
            for flow in flows:
                flow.append(lax.ppermute(flow[-1], "blk", onward))
        own, _, sent, sent_lent = form(doc_inputs, doc_outgrads, token_mask, spot, stay)
        far, far_lent = swap_across(sent), swap_across(sent_lent)
        for step in range(places):
            first, second = flows[0][step], flows[1][step]
            keep, give = score(
                own_body, stay, spot, (own, far, far_lent, first, second, first, second), docs, queries, ()
            )
            total, _ = take(keep, give, swap_across, swap_cores)
            origin = (place - step + places) % places
            out = lax.dynamic_update_slice_in_dim(out, total, origin * (2 * queries), 1)
        return out

    def at(place):
        return [2 * place, 2 * place + 1]

    inward = list(zip(at(0) + at(3), at(1) + at(2)))
    outward = [(b, a) for a, b in inward]
    centre = list(zip(at(1) + at(2), at(2) + at(1)))
    inner_across = [(b, b ^ 1) for b in at(1) + at(2)]
    inner_cores = [(2 * b + c, 2 * b + 1 - c) for b in at(1) + at(2) for c in range(2)]

    def move(x, pairs):
        return lax.ppermute(x, "blk", pairs)

    def staying(x):
        return x[:, :stay]

    mate_a = move(mine, inward)
    near_a = move(mine, centre)
    outer_mate_a = move(mine_stay, outward)
    own, lent, sent, sent_lent = form(doc_inputs, doc_outgrads, token_mask, spot, stay, outer_mate_a)
    sent, sent_lent = tie((sent, sent_lent), mate_a, near_a, other)

    far_lent = swap_across(sent_lent)
    far = swap_across(sent)
    mate_b = move(other, inward)
    near_b = move(other, centre)
    outer_near_a = move(staying(near_a), outward)
    outer_mate_b = move(staying(other), outward)
    lent, far_lent = tie((lent, far_lent), mate_b, near_b, outer_near_a)

    lent_near = move(lent, inward)
    lent_far = move(far_lent, inward)
    away_a = move(mate_a, centre)
    outer_near_b = move(staying(near_b), outward)
    outer_away_a = move(staying(away_a), outward)
    away_b = move(mate_b, centre)
    outer_away_b = move(staying(away_b), outward)

    groups = {
        "self": (mine, other, mine, other),
        "mate": (mate_a, mate_b, outer_mate_a, outer_mate_b),
        "near": (near_a, near_b, outer_near_a, outer_near_b),
        "away": (away_a, away_b, outer_away_a, outer_away_b),
    }
    opposite = place < 2
    origins = {
        "self": place,
        "mate": place ^ 1,
        "near": jnp.where(opposite, 2, 1),
        "away": jnp.where(opposite, 3, 0),
    }

    def own_part(name, *after):
        return score(own_body, stay, spot, (own, far, far_lent) + groups[name], docs, queries, after)

    def lent_part(name, *after):
        return score(lent_body, stay, spot, (lent_near, lent_far) + groups[name][:2], docs, queries, after)

    def back(keep, give):
        total, beside = take(
            keep, give, lambda x: move(x, inner_across), lambda x: lax.ppermute(x, ("blk", "proj"), inner_cores)
        )
        return move(total.astype(bf16), outward), beside

    totals, besides, returned = {}, {}, {}

    last = (away_a, outer_mate_b, outer_near_b)
    for name in ("self", "near", "mate"):
        k, g = own_part(name, *last)
        totals[name], besides[name] = take(k, g, swap_across, swap_cores)
        last = (g,)
    forced = {"self": outer_away_a, "near": besides["self"], "mate": besides["near"], "away": besides["mate"]}
    for name in ("self", "near", "mate", "away"):
        k, g = lent_part(name, *last, forced[name])
        returned[name], _ = back(k, g)
        last = (g,)
    k, g = own_part("away", *last)
    totals["away"], _ = take(k, g, swap_across, swap_cores)
    backs = {"self": "mate", "mate": "self", "near": "near", "away": "away"}
    for name in ("self", "near", "mate", "away"):
        total = totals[name] + returned[backs[name]].astype(f32)
        out = lax.dynamic_update_slice_in_dim(out, total, origins[name] * (2 * queries), 1)
    return out


def solution(mesh):
    placed = (
        P(("grp", "blk"), "proj", None, None),
        P(("grp", "blk"), "proj", None, None),
        P(("grp", "blk"), None),
        P(("grp", "blk"), "proj"),
    )
    return jax.shard_map(
        on_device,
        mesh=mesh,
        in_specs=placed,
        out_specs=P(("grp", "blk", "proj"), None),
        check_vma=False,
    )
```

```python
import functools

import jax
import jax.numpy as jnp
from jax import lax
from jax.experimental import pallas as pl
from jax.experimental.pallas import tpu as pltpu
from jax.sharding import PartitionSpec as P

LANES = 128
VMEM_LIMIT = 48 * 1024 * 1024
ANYWHERE = pl.BlockSpec(memory_space=pl.ANY)
SCALARS = pl.BlockSpec(memory_space=pltpu.SMEM)
WHOLE = pl.BlockSpec(memory_space=pltpu.VMEM)
NT = (((1,), (1,)), ((), ()))
bf16, f32 = jnp.bfloat16, jnp.float32
LIMIT = pltpu.CompilerParams(vmem_limit_bytes=VMEM_LIMIT)


def shaped(kind, *shape):
    return jax.ShapeDtypeStruct(shape, kind)


def prepare_body(spot, query_grads, mine, start, other):
    rank = LANES // 2
    width = query_grads.shape[1]
    for outs, side in (((mine, start), spot[0]), ((other,), 1 - spot[0])):
        for m in range(width // 4 // LANES):
            at = pl.multiple_of(side * (width // 4) + m * LANES, LANES)
            low = query_grads[:, pl.ds(at, LANES)]
            high = query_grads[:, pl.ds(at + width // 2, LANES)]
            for odd, block in enumerate((
                jnp.concatenate([low[:, :rank], high[:, :rank]], 1),
                jnp.concatenate([low[:, rank:], high[:, rank:]], 1),
            )):
                k = 2 * m + odd
                for out in outs:
                    if k * LANES < out.shape[1]:
                        out[:, k * LANES:(k + 1) * LANES] = block


def prepare(query_grads, spot, stay):
    rows, width = query_grads.shape
    return pl.pallas_call(
        prepare_body,
        in_specs=[SCALARS, WHOLE],
        out_specs=[WHOLE] * 3,
        out_shape=[shaped(bf16, rows, width // 2), shaped(bf16, rows, stay), shaped(bf16, rows, width // 2)],
        compiler_params=LIMIT,
    )(spot, query_grads)


def form_body(rows, rank, spot, inputs, outgrads, mask, *refs):
    kept, lent, sent, sent_lent, rounds = refs[-5:]
    for d in range(rows):
        masked = outgrads[d] * mask[d:d + 1, :].astype(bf16)
        product = lax.dot_general(inputs[d], masked, NT, preferred_element_type=f32)
        pairs = jnp.concatenate([product[:rank // 2], product[rank // 2:]], 1)
        rounds[pl.ds(d, rank // 2, stride=rows), :] = pairs
    stay = sent.shape[1] // LANES
    for which in range(2):
        side = spot[0] if which == 0 else 1 - spot[0]
        for k in range(rank // 4):
            at = pl.multiple_of((side * (rank // 4) + k) * rows, rows)
            block = rounds[pl.ds(at, rows), :].astype(bf16)
            if which == 0:
                kept[:, k * LANES:(k + 1) * LANES] = block
                if k >= stay:
                    lent[:, (k - stay) * LANES:(k - stay + 1) * LANES] = block
            elif k < stay:
                sent[:, k * LANES:(k + 1) * LANES] = block
            else:
                sent_lent[:, (k - stay) * LANES:(k - stay + 1) * LANES] = block


def form(doc_inputs, doc_outgrads, token_mask, spot, stay, *after):
    docs, rank, length = doc_inputs.shape
    rows = 64
    steps = docs // rows
    half = rank * rank // 2
    widths = (half, half - stay, stay, half - stay)

    def at(g, spot):
        return lax.rem(g + spot[1] * (steps // 2), steps)

    return pl.pallas_call(
        functools.partial(form_body, rows, rank),
        grid_spec=pltpu.PrefetchScalarGridSpec(
            num_scalar_prefetch=1,
            grid=(steps,),
            in_specs=[
                pl.BlockSpec((rows, rank, length), lambda g, spot: (at(g, spot), 0, 0)),
                pl.BlockSpec((rows, rank, length), lambda g, spot: (at(g, spot), 0, 0)),
                pl.BlockSpec((rows, length), lambda g, spot: (at(g, spot), 0)),
            ] + [ANYWHERE] * len(after),
            out_specs=[pl.BlockSpec((rows, width), lambda g, spot: (g, 0)) for width in widths],
            scratch_shapes=[pltpu.VMEM((rank // 2 * rows, LANES), f32)],
        ),
        out_shape=[shaped(bf16, docs, width) for width in widths],
        compiler_params=LIMIT,
        cost_estimate=pl.CostEstimate(
            flops=40 * docs * rank * rank * length, bytes_accessed=4 * docs * rank * length + 2 * docs * rank * rank, transcendentals=0
        ),
    )(spot, doc_inputs, doc_outgrads, token_mask, *after)


def tie(arrays, *after):
    count = len(arrays)
    return pl.pallas_call(
        lambda *refs: None,
        in_specs=[ANYWHERE] * (count + len(after)),
        out_specs=[ANYWHERE] * count,
        out_shape=[shaped(a.dtype, *a.shape) for a in arrays],
        input_output_aliases={i: i for i in range(count)},
        compiler_params=LIMIT,
    )(*arrays, *after)


def store_products(spot, blocks, rows_of, keep, give):
    part = keep.shape[0] // 2
    queries = blocks[0].shape[0]
    for block, slot in zip(blocks, (spot[0], 1 - spot[0])):
        at = pl.ds(pl.multiple_of(slot * queries, queries), queries)
        products = rows_of(block)
        keep[:part, at] = products[0]
        give[:part, at] = products[1].astype(bf16)
        keep[part:, at] = products[2]
        give[part:, at] = products[3].astype(bf16)


def dot(rows, block):
    return lax.dot_general(rows, block, NT, preferred_element_type=f32)


def own_body(stay, spot, own, far, far_lent, first, second, first_stay, second_stay, *refs):
    keep, give = refs[-2:]
    part = own.shape[0] // 2

    def all_features(block):
        out = []
        for h in range(2):
            out.append(dot(own[h * part:(h + 1) * part, :], block[...]))
        for h in range(2):
            rows = slice(h * part, (h + 1) * part)
            out.append(dot(far[rows, :], block[:, :stay]) + dot(far_lent[rows, :], block[:, stay:]))
        return out

    def staying(block):
        out = []
        for h in range(2):
            out.append(dot(own[h * part:(h + 1) * part, :stay], block[:, :stay]))
        for h in range(2):
            out.append(dot(far[h * part:(h + 1) * part, :], block[:, :stay]))
        return out

    @pl.when(spot[2] == 1)
    def _():
        store_products(spot, (first, second), all_features, keep, give)

    @pl.when(spot[2] == 0)
    def _():
        store_products(spot, (first_stay, second_stay), staying, keep, give)


def lent_body(stay, spot, near, far, first, second, *refs):
    keep, give = refs[-2:]
    part = near.shape[0] // 2

    def products(block):
        return [
            dot(rows[h * part:(h + 1) * part, :], block[:, stay:]) for rows in (near, far) for h in range(2)
        ]

    @pl.when(spot[2] == 1)
    def _():
        store_products(spot, (first, second), products, keep, give)


def score(body, stay, spot, operands, docs, queries, after):
    return pl.pallas_call(
        functools.partial(body, stay),
        in_specs=[SCALARS] + [WHOLE] * len(operands) + [ANYWHERE] * len(after),
        out_specs=[WHOLE] * 2,
        out_shape=[shaped(f32, docs, 2 * queries), shaped(bf16, docs, 2 * queries)],
        compiler_params=LIMIT,
        cost_estimate=pl.CostEstimate(flops=docs * queries, bytes_accessed=docs * queries, transcendentals=0),
    )(spot, *operands, *after)


def on_device(doc_inputs, doc_outgrads, token_mask, query_grads):
    blk = lax.axis_size("blk")
    places = blk // 2
    me = lax.axis_index("blk")
    place, side = me // 2, me % 2
    docs, rank = doc_inputs.shape[0], doc_inputs.shape[2]
    queries = query_grads.shape[0]
    part = docs // 2
    half = rank * rank // 2
    doc_inputs = doc_inputs.reshape(docs, *doc_inputs.shape[2:])
    doc_outgrads = doc_outgrads.reshape(docs, *doc_outgrads.shape[2:])
    lending = places == 4
    stay = half * 10 // 16
    inner = jnp.where((place == 1) | (place == 2), 1, 0) if lending else 1
    spot = jnp.stack([side, lax.axis_index("proj"), inner]).astype(jnp.int32)

    across = [(b, b ^ 1) for b in range(blk)]
    onward = [(b, (b + 2) % blk) for b in range(blk)]
    cores = [(0, 1), (1, 0)]

    mine, mine_stay, sending = prepare(query_grads, spot, stay)
    other = lax.ppermute(sending, "blk", across)

    def take(keep, give, far_across, far_cores):
        got = far_cores(give)
        beside = far_across((keep[part:] + got[part:].astype(f32)).astype(bf16))
        return keep[:part] + got[:part].astype(f32) + beside.astype(f32), beside

    def swap_across(x):
        return lax.ppermute(x, "blk", across)

    def swap_cores(x):
        return lax.ppermute(x, "proj", cores)

    out = jnp.zeros((part, blk * queries), f32)
    if not lending:
        flows = [[mine], [other]]
        for step in range(1, places):
            for flow in flows:
                flow.append(lax.ppermute(flow[-1], "blk", onward))
        own, _, sent, sent_lent = form(doc_inputs, doc_outgrads, token_mask, spot, stay)
        far, far_lent = swap_across(sent), swap_across(sent_lent)
        for step in range(places):
            first, second = flows[0][step], flows[1][step]
            keep, give = score(
                own_body, stay, spot, (own, far, far_lent, first, second, first, second), docs, queries, ()
            )
            total, _ = take(keep, give, swap_across, swap_cores)
            origin = (place - step + places) % places
            out = lax.dynamic_update_slice_in_dim(out, total, origin * (2 * queries), 1)
        return out

    def at(place):
        return [2 * place, 2 * place + 1]

    inward = list(zip(at(0) + at(3), at(1) + at(2)))
    outward = [(b, a) for a, b in inward]
    centre = list(zip(at(1) + at(2), at(2) + at(1)))
    inner_across = [(b, b ^ 1) for b in at(1) + at(2)]
    inner_cores = [(2 * b + c, 2 * b + 1 - c) for b in at(1) + at(2) for c in range(2)]

    def move(x, pairs):
        return lax.ppermute(x, "blk", pairs)

    def staying(x):
        return x[:, :stay]

    mate_a = move(mine, inward)
    near_a = move(mine, centre)
    outer_mate_a = move(mine_stay, outward)
    own, lent, sent, sent_lent = form(doc_inputs, doc_outgrads, token_mask, spot, stay)
    sent, sent_lent, mate_a, near_a, other = tie((sent, sent_lent, mate_a, near_a, other), outer_mate_a)

    far_lent = swap_across(sent_lent)
    far = swap_across(sent)
    mate_b = move(other, inward)
    near_b = move(other, centre)
    outer_near_a = move(staying(near_a), outward)
    outer_mate_b = move(staying(other), outward)
    lent, far_lent = tie((lent, far_lent), mate_b, near_b, outer_near_a)

    lent_near = move(lent, inward)
    lent_far = move(far_lent, inward)
    away_a = move(mate_a, centre)
    outer_near_b = move(staying(near_b), outward)
    outer_away_a = move(staying(away_a), outward)
    away_b = move(mate_b, centre)
    outer_away_b = move(staying(away_b), outward)

    groups = {
        "self": (mine, other, mine, other),
        "mate": (mate_a, mate_b, outer_mate_a, outer_mate_b),
        "near": (near_a, near_b, outer_near_a, outer_near_b),
        "away": (away_a, away_b, outer_away_a, outer_away_b),
    }
    opposite = place < 2
    origins = {
        "self": place,
        "mate": place ^ 1,
        "near": jnp.where(opposite, 2, 1),
        "away": jnp.where(opposite, 3, 0),
    }

    def own_part(name, *after):
        return score(own_body, stay, spot, (own, far, far_lent) + groups[name], docs, queries, after)

    def lent_part(name, *after):
        return score(lent_body, stay, spot, (lent_near, lent_far) + groups[name][:2], docs, queries, after)

    def back(keep, give):
        total, beside = take(
            keep, give, lambda x: move(x, inner_across), lambda x: lax.ppermute(x, ("blk", "proj"), inner_cores)
        )
        return move(total.astype(bf16), outward), beside

    totals, besides, returned = {}, {}, {}

    last = (away_a, outer_mate_b, outer_near_b)
    for name in ("self", "near", "mate"):
        k, g = own_part(name, *last)
        totals[name], besides[name] = take(k, g, swap_across, swap_cores)
        last = (g,)
    forced = {"self": outer_away_a, "near": besides["self"], "mate": besides["near"], "away": besides["mate"]}
    for name in ("self", "near", "mate", "away"):
        k, g = lent_part(name, *last, forced[name])
        returned[name], _ = back(k, g)
        last = (g,)
    k, g = own_part("away", *last)
    totals["away"], _ = take(k, g, swap_across, swap_cores)
    backs = {"self": "mate", "mate": "self", "near": "near", "away": "away"}
    for name in ("self", "near", "mate", "away"):
        total = totals[name] + returned[backs[name]].astype(f32)
        out = lax.dynamic_update_slice_in_dim(out, total, origins[name] * (2 * queries), 1)
    return out


def solution(mesh):
    placed = (
        P(("grp", "blk"), "proj", None, None),
        P(("grp", "blk"), "proj", None, None),
        P(("grp", "blk"), None),
        P(("grp", "blk"), "proj"),
    )
    return jax.shard_map(
        on_device,
        mesh=mesh,
        in_specs=placed,
        out_specs=P(("grp", "blk", "proj"), None),
        check_vma=False,
    )
```

```python
import functools

import jax
import jax.numpy as jnp
from jax import lax
from jax.experimental import pallas as pl
from jax.experimental.pallas import tpu as pltpu
from jax.sharding import PartitionSpec as P

LANES = 128
VMEM_LIMIT = 48 * 1024 * 1024
ANYWHERE = pl.BlockSpec(memory_space=pl.ANY)
SCALARS = pl.BlockSpec(memory_space=pltpu.SMEM)
WHOLE = pl.BlockSpec(memory_space=pltpu.VMEM)
NT = (((1,), (1,)), ((), ()))
bf16, f32 = jnp.bfloat16, jnp.float32
LIMIT = pltpu.CompilerParams(vmem_limit_bytes=VMEM_LIMIT)


def shaped(kind, *shape):
    return jax.ShapeDtypeStruct(shape, kind)


def prepare_body(spot, query_grads, mine, other):
    rank = LANES // 2
    width = query_grads.shape[1]
    for out, side in ((mine, spot[0]), (other, 1 - spot[0])):
        for m in range(width // 4 // LANES):
            at = pl.multiple_of(side * (width // 4) + m * LANES, LANES)
            low = query_grads[:, pl.ds(at, LANES)]
            high = query_grads[:, pl.ds(at + width // 2, LANES)]
            out[:, 2 * m * LANES:(2 * m + 1) * LANES] = jnp.concatenate([low[:, :rank], high[:, :rank]], 1)
            out[:, (2 * m + 1) * LANES:(2 * m + 2) * LANES] = jnp.concatenate([low[:, rank:], high[:, rank:]], 1)


def prepare(query_grads, spot):
    rows, width = query_grads.shape
    return pl.pallas_call(
        prepare_body,
        in_specs=[SCALARS, WHOLE],
        out_specs=[WHOLE] * 2,
        out_shape=[shaped(bf16, rows, width // 2)] * 2,
        compiler_params=LIMIT,
    )(spot, query_grads)


def form_body(rows, rank, spot, inputs, outgrads, mask, kept, sent, rounds):
    for d in range(rows):
        masked = outgrads[d] * mask[d:d + 1, :].astype(bf16)
        product = lax.dot_general(inputs[d], masked, NT, preferred_element_type=f32)
        pairs = jnp.concatenate([product[:rank // 2], product[rank // 2:]], 1)
        rounds[pl.ds(d, rank // 2, stride=rows), :] = pairs
    for out, side in ((kept, spot[0]), (sent, 1 - spot[0])):
        for k in range(rank // 4):
            at = pl.multiple_of((side * (rank // 4) + k) * rows, rows)
            out[:, k * LANES:(k + 1) * LANES] = rounds[pl.ds(at, rows), :].astype(bf16)


def form(doc_inputs, doc_outgrads, token_mask, spot):
    docs, rank, length = doc_inputs.shape
    rows = 64
    steps = docs // rows
    half = rank * rank // 2

    def at(g, spot):
        return lax.rem(g + spot[1] * (steps // 2), steps)

    return pl.pallas_call(
        functools.partial(form_body, rows, rank),
        grid_spec=pltpu.PrefetchScalarGridSpec(
            num_scalar_prefetch=1,
            grid=(steps,),
            in_specs=[
                pl.BlockSpec((rows, rank, length), lambda g, spot: (at(g, spot), 0, 0)),
                pl.BlockSpec((rows, rank, length), lambda g, spot: (at(g, spot), 0, 0)),
                pl.BlockSpec((rows, length), lambda g, spot: (at(g, spot), 0)),
            ],
            out_specs=[pl.BlockSpec((rows, half), lambda g, spot: (g, 0))] * 2,
            scratch_shapes=[pltpu.VMEM((rank // 2 * rows, LANES), f32)],
        ),
        out_shape=[shaped(bf16, docs, half)] * 2,
        compiler_params=LIMIT,
        cost_estimate=pl.CostEstimate(
            flops=40 * docs * rank * rank * length, bytes_accessed=4 * docs * rank * length + 2 * docs * rank * rank, transcendentals=0
        ),
    )(spot, doc_inputs, doc_outgrads, token_mask)


def tie(arrays, *after):
    count = len(arrays)
    return pl.pallas_call(
        lambda *refs: None,
        in_specs=[ANYWHERE] * (count + len(after)),
        out_specs=[ANYWHERE] * count,
        out_shape=[shaped(a.dtype, *a.shape) for a in arrays],
        input_output_aliases={i: i for i in range(count)},
        compiler_params=LIMIT,
    )(*arrays, *after)


def dot(rows, block):
    return lax.dot_general(rows, block, NT, preferred_element_type=f32)


FREE = pl.CostEstimate(flops=1024, bytes_accessed=1024, transcendentals=0)


def score_body(count, spot, own, far, *refs):
    keep, give = refs[-2:]
    part = own.shape[0] // 2
    blocks = refs[:count]
    queries = blocks[0].shape[0]
    slots = (spot[0], 1 - spot[0]) if count == 2 else (0,)
    for block, slot in zip(blocks, slots):
        at = pl.ds(pl.multiple_of(slot * queries, queries), queries) if count == 2 else slice(None)
        keep[:part, at] = dot(own[:part, :], block[...])
        keep[part:, at] = dot(far[:part, :], block[...])
        give[:part, at] = dot(own[part:, :], block[...]).astype(bf16)
        give[part:, at] = dot(far[part:, :], block[...]).astype(bf16)


def score(spot, own, far, blocks, *after):
    docs = own.shape[0]
    count = len(blocks)
    queries = count * blocks[0].shape[0]
    return pl.pallas_call(
        functools.partial(score_body, count),
        in_specs=[SCALARS] + [WHOLE] * (2 + count) + [ANYWHERE] * len(after),
        out_specs=[WHOLE] * 2,
        out_shape=[shaped(f32, docs, queries), shaped(bf16, docs, queries)],
        compiler_params=LIMIT,
        cost_estimate=FREE,
    )(spot, own, far, *blocks, *after)


def last_body(own, far, block, *refs):
    near, mate, across, diagonal = refs[-4:]
    part = near.shape[0]
    mate[...] = dot(own[part:, :], block[...]).astype(bf16)
    across[...] = dot(far[:part, :], block[...]).astype(bf16)
    diagonal[...] = dot(far[part:, :], block[...]).astype(bf16)
    near[...] = dot(own[:part, :], block[...])


def last_score(own, far, block, *after):
    shape = (own.shape[0] // 2, block.shape[0])
    return pl.pallas_call(
        last_body,
        in_specs=[WHOLE] * 3 + [ANYWHERE] * len(after),
        out_specs=[WHOLE] * 4,
        out_shape=[shaped(f32, *shape)] + [shaped(bf16, *shape)] * 3,
        compiler_params=LIMIT,
        cost_estimate=FREE,
    )(own, far, block, *after)


def on_device(doc_inputs, doc_outgrads, token_mask, query_grads):
    blk = lax.axis_size("blk")
    places = blk // 2
    me = lax.axis_index("blk")
    place, side = me // 2, me % 2
    spot = jnp.stack([side, lax.axis_index("proj")]).astype(jnp.int32)
    docs = doc_inputs.shape[0]
    queries = query_grads.shape[0]
    part = docs // 2

    across = [(b, b ^ 1) for b in range(blk)]
    onward = [(b, (b + 2) % blk) for b in range(blk)]
    diagonal = [(2 * b + c, 2 * (b ^ 1) + (c ^ 1)) for b in range(blk) for c in range(2)]

    def swap_across(x):
        return lax.ppermute(x, "blk", across)

    def swap_cores(x):
        return lax.ppermute(x, "proj", [(0, 1), (1, 0)])

    def pass_on(x):
        return lax.ppermute(x, "blk", onward)

    def swap_diagonal(x):
        return lax.ppermute(x, ("blk", "proj"), diagonal)

    mine, sending = prepare(query_grads, spot)
    other = swap_across(sending)
    first = [mine, pass_on(mine)]
    own, sent = form(
        doc_inputs.reshape(docs, *doc_inputs.shape[2:]), doc_outgrads.reshape(docs, *doc_outgrads.shape[2:]), token_mask, spot
    )
    sent, first[1], other = tie((sent, first[1], other))
    second = [other]
    far = swap_across(sent)
    for step in range(2, places):
        first.append(pass_on(first[-1]))
    for step in range(1, places - 1):
        second.append(pass_on(second[-1]))
    pieces = [pass_on(piece) for piece in jnp.split(second[-1], 2, 0)]

    out = jnp.zeros((part, blk * queries), f32)

    def put(out, total, step, at):
        origin = (place - step + places) % places
        return lax.dynamic_update_slice_in_dim(out, total, origin * (2 * queries) + at, 1)

    def over_cores(keep, give):
        got = swap_cores(give).astype(f32)
        return keep[:part] + got[:part], (keep[part:] + got[part:]).astype(bf16)

    besides = []
    last = ()
    for step in range(places - 1):
        if step == places - 2:
            keep, give = score(spot, own, far, (first[-1],), *last)
            final_own, final_far = over_cores(keep, give)
            final_beside = swap_across(final_far)
            last = (give,) + tuple(besides)
        keep, give = score(spot, own, far, (first[step], second[step]), *last)
        total, reach = over_cores(keep, give)
        besides.append(swap_across(reach))
        out = put(out, total + besides[-1].astype(f32), step, 0)
        last = (give,)
    last = (give, final_beside)

    size = queries // 2
    for i, piece in enumerate(pieces):
        near, mate, reach, opposite = last_score(own, far, piece, *last)
        cut = slice(i * size, (i + 1) * size)
        mine_total = final_own[:, cut] + swap_across(reach).astype(f32) + swap_diagonal(opposite).astype(f32)
        other_total = near + swap_cores(mate).astype(f32) + final_beside[:, cut].astype(f32)
        out = put(out, mine_total, places - 1, side * queries + i * size)
        out = put(out, other_total, places - 1, (1 - side) * queries + i * size)
        last = (near, besides[-1])
    return out


def solution(mesh):
    placed = (
        P(("grp", "blk"), "proj", None, None),
        P(("grp", "blk"), "proj", None, None),
        P(("grp", "blk"), None),
        P(("grp", "blk"), "proj"),
    )
    return jax.shard_map(
        on_device,
        mesh=mesh,
        in_specs=placed,
        out_specs=P(("grp", "blk", "proj"), None),
        check_vma=False,
    )
```

```python
import functools

import jax
import jax.numpy as jnp
from jax import lax
from jax.experimental import pallas as pl
from jax.experimental.pallas import tpu as pltpu
from jax.sharding import PartitionSpec as P

LANES = 128
VMEM_LIMIT = 48 * 1024 * 1024
ANYWHERE = pl.BlockSpec(memory_space=pl.ANY)
SCALARS = pl.BlockSpec(memory_space=pltpu.SMEM)
WHOLE = pl.BlockSpec(memory_space=pltpu.VMEM)
NT = (((1,), (1,)), ((), ()))
bf16, f32 = jnp.bfloat16, jnp.float32
LIMIT = pltpu.CompilerParams(vmem_limit_bytes=VMEM_LIMIT)


def shaped(kind, *shape):
    return jax.ShapeDtypeStruct(shape, kind)


def prepare_body(spot, query_grads, mine, *sending):
    rank = LANES // 2
    rows, width = query_grads.shape
    for outs, side in (((mine,), spot[0]), (sending, 1 - spot[0])):
        for m in range(width // 4 // LANES):
            at = pl.multiple_of(side * (width // 4) + m * LANES, LANES)
            low = query_grads[:, pl.ds(at, LANES)]
            high = query_grads[:, pl.ds(at + width // 2, LANES)]
            even = jnp.concatenate([low[:, :rank], high[:, :rank]], 1)
            odd = jnp.concatenate([low[:, rank:], high[:, rank:]], 1)
            for i, out in enumerate(outs):
                cut = slice(i * out.shape[0], (i + 1) * out.shape[0])
                out[:, 2 * m * LANES:(2 * m + 1) * LANES] = even[cut, :]
                out[:, (2 * m + 1) * LANES:(2 * m + 2) * LANES] = odd[cut, :]


def prepare(query_grads, spot):
    rows, width = query_grads.shape
    return pl.pallas_call(
        prepare_body,
        in_specs=[SCALARS, WHOLE],
        out_specs=[WHOLE] * 3,
        out_shape=[shaped(bf16, size, width // 2) for size in (rows, rows // 2, rows // 2)],
        compiler_params=LIMIT,
    )(spot, query_grads)


def form_body(rows, rank, spot, inputs, outgrads, mask, kept, sent, rounds):
    for d in range(rows):
        masked = outgrads[d] * mask[d:d + 1, :].astype(bf16)
        product = lax.dot_general(inputs[d], masked, NT, preferred_element_type=f32)
        pairs = jnp.concatenate([product[:rank // 2], product[rank // 2:]], 1)
        rounds[pl.ds(d, rank // 2, stride=rows), :] = pairs
    for out, side in ((kept, spot[0]), (sent, 1 - spot[0])):
        for k in range(rank // 4):
            at = pl.multiple_of((side * (rank // 4) + k) * rows, rows)
            out[:, k * LANES:(k + 1) * LANES] = rounds[pl.ds(at, rows), :].astype(bf16)


def form(doc_inputs, doc_outgrads, token_mask, spot):
    docs, rank, length = doc_inputs.shape
    rows = 64
    steps = docs // rows
    half = rank * rank // 2

    def at(g, spot):
        return lax.rem(g + spot[1] * (steps // 2), steps)

    return pl.pallas_call(
        functools.partial(form_body, rows, rank),
        grid_spec=pltpu.PrefetchScalarGridSpec(
            num_scalar_prefetch=1,
            grid=(steps,),
            in_specs=[
                pl.BlockSpec((rows, rank, length), lambda g, spot: (at(g, spot), 0, 0)),
                pl.BlockSpec((rows, rank, length), lambda g, spot: (at(g, spot), 0, 0)),
                pl.BlockSpec((rows, length), lambda g, spot: (at(g, spot), 0)),
            ],
            out_specs=[pl.BlockSpec((rows, half), lambda g, spot: (g, 0))] * 2,
            scratch_shapes=[pltpu.VMEM((rank // 2 * rows, LANES), f32)],
        ),
        out_shape=[shaped(bf16, docs, half)] * 2,
        compiler_params=LIMIT,
        cost_estimate=pl.CostEstimate(
            flops=40 * docs * rank * rank * length, bytes_accessed=4 * docs * rank * length + 2 * docs * rank * rank, transcendentals=0
        ),
    )(spot, doc_inputs, doc_outgrads, token_mask)


def tie(arrays, *after):
    count = len(arrays)
    return pl.pallas_call(
        lambda *refs: None,
        in_specs=[ANYWHERE] * (count + len(after)),
        out_specs=[ANYWHERE] * count,
        out_shape=[shaped(a.dtype, *a.shape) for a in arrays],
        input_output_aliases={i: i for i in range(count)},
        compiler_params=LIMIT,
    )(*arrays, *after)


def dot(rows, block):
    return lax.dot_general(rows, block, NT, preferred_element_type=f32)


FREE = pl.CostEstimate(flops=1024, bytes_accessed=1024, transcendentals=0)


def score_body(count, spot, own, far, *refs):
    keep, give = refs[-2:]
    part = own.shape[0] // 2
    rows = refs[0].shape[0]
    for i, block in enumerate(refs[:count]):
        size = block.shape[0]
        if count == 1:
            at = slice(None)
        elif i == 0:
            at = pl.ds(pl.multiple_of(spot[0] * rows, rows), size)
        else:
            at = pl.ds(pl.multiple_of((1 - spot[0]) * rows + (i - 1) * size, size), size)
        keep[:part, at] = dot(own[:part, :], block[...])
        keep[part:, at] = dot(far[:part, :], block[...])
        give[:part, at] = dot(own[part:, :], block[...]).astype(bf16)
        give[part:, at] = dot(far[part:, :], block[...]).astype(bf16)


def score(spot, own, far, blocks, *after):
    docs = own.shape[0]
    count = len(blocks)
    queries = sum(block.shape[0] for block in blocks)
    return pl.pallas_call(
        functools.partial(score_body, count),
        in_specs=[SCALARS] + [WHOLE] * (2 + count) + [ANYWHERE] * len(after),
        out_specs=[WHOLE] * 2,
        out_shape=[shaped(f32, docs, queries), shaped(bf16, docs, queries)],
        compiler_params=LIMIT,
        cost_estimate=FREE,
    )(spot, own, far, *blocks, *after)


def last_body(own, far, block, *refs):
    near, mate, across, diagonal = refs[-4:]
    part = near.shape[0]
    mate[...] = dot(own[part:, :], block[...]).astype(bf16)
    across[...] = dot(far[:part, :], block[...]).astype(bf16)
    diagonal[...] = dot(far[part:, :], block[...]).astype(bf16)
    near[...] = dot(own[:part, :], block[...])


def last_score(own, far, block, *after):
    shape = (own.shape[0] // 2, block.shape[0])
    return pl.pallas_call(
        last_body,
        in_specs=[WHOLE] * 3 + [ANYWHERE] * len(after),
        out_specs=[WHOLE] * 4,
        out_shape=[shaped(f32, *shape)] + [shaped(bf16, *shape)] * 3,
        compiler_params=LIMIT,
        cost_estimate=FREE,
    )(own, far, block, *after)


def on_device(doc_inputs, doc_outgrads, token_mask, query_grads):
    blk = lax.axis_size("blk")
    places = blk // 2
    me = lax.axis_index("blk")
    place, side = me // 2, me % 2
    spot = jnp.stack([side, lax.axis_index("proj")]).astype(jnp.int32)
    docs = doc_inputs.shape[0]
    queries = query_grads.shape[0]
    part = docs // 2

    across = [(b, b ^ 1) for b in range(blk)]
    onward = [(b, (b + 2) % blk) for b in range(blk)]
    diagonal = [(2 * b + c, 2 * (b ^ 1) + (c ^ 1)) for b in range(blk) for c in range(2)]

    def swap_across(x):
        return lax.ppermute(x, "blk", across)

    def swap_cores(x):
        return lax.ppermute(x, "proj", [(0, 1), (1, 0)])

    def pass_on(x):
        return lax.ppermute(x, "blk", onward)

    def swap_diagonal(x):
        return lax.ppermute(x, ("blk", "proj"), diagonal)

    mine, *sending = prepare(query_grads, spot)
    ahead = pass_on(mine)
    other = [swap_across(x) for x in sending]
    own, sent = form(
        doc_inputs.reshape(docs, *doc_inputs.shape[2:]), doc_outgrads.reshape(docs, *doc_outgrads.shape[2:]), token_mask, spot
    )
    sent, ahead, *other = tie((sent, ahead, *other))
    far = swap_across(sent)
    first, second = [mine, ahead], [other]
    for step in range(2, places):
        first.append(pass_on(first[-1]))
    for step in range(1, places):
        second.append([pass_on(x) for x in second[-1]])
    pieces = second[-1]

    out = jnp.zeros((part, blk * queries), f32)

    def put(out, total, step, at):
        origin = (place - step + places) % places
        return lax.dynamic_update_slice_in_dim(out, total, origin * (2 * queries) + at, 1)

    def over_cores(keep, give):
        got = swap_cores(give).astype(f32)
        return keep[:part] + got[:part], (keep[part:] + got[part:]).astype(bf16)

    besides = []
    last = ()
    for step in range(places - 1):
        if step == places - 2:
            keep, give = score(spot, own, far, [first[-1]], *last)
            final_own, final_far = over_cores(keep, give)
            final_beside = swap_across(final_far)
            last = (give,) + tuple(besides)
        keep, give = score(spot, own, far, [first[step]] + second[step], *last)
        total, reach = over_cores(keep, give)
        besides.append(swap_across(reach))
        out = put(out, total + besides[-1].astype(f32), step, 0)
        last = (give,)
    last = (give,)

    size = queries // 2
    for i, piece in enumerate(pieces):
        near, give, facing, opposite = last_score(own, far, piece, *last)
        cut = slice(i * size, (i + 1) * size)
        mine_total = final_own[:, cut] + swap_across(facing).astype(f32) + swap_diagonal(opposite).astype(f32)
        other_total = near + swap_cores(give).astype(f32) + final_beside[:, cut].astype(f32)
        out = put(out, mine_total, places - 1, side * queries + i * size)
        out = put(out, other_total, places - 1, (1 - side) * queries + i * size)
        last = (near, final_beside, reach)
    return out


def solution(mesh):
    placed = (
        P(("grp", "blk"), "proj", None, None),
        P(("grp", "blk"), "proj", None, None),
        P(("grp", "blk"), None),
        P(("grp", "blk"), "proj"),
    )
    return jax.shard_map(
        on_device,
        mesh=mesh,
        in_specs=placed,
        out_specs=P(("grp", "blk", "proj"), None),
        check_vma=False,
    )
```

```python
import functools

import jax
import jax.numpy as jnp
from jax import lax
from jax.experimental import pallas as pl
from jax.experimental.pallas import tpu as pltpu
from jax.sharding import PartitionSpec as P

LANES = 128
LENT = 6
VMEM_LIMIT = 48 * 1024 * 1024
ANYWHERE = pl.BlockSpec(memory_space=pl.ANY)
SCALARS = pl.BlockSpec(memory_space=pltpu.SMEM)
WHOLE = pl.BlockSpec(memory_space=pltpu.VMEM)
NT = (((1,), (1,)), ((), ()))
bf16, f32 = jnp.bfloat16, jnp.float32
LIMIT = pltpu.CompilerParams(vmem_limit_bytes=VMEM_LIMIT)
FREE = pl.CostEstimate(flops=1024, bytes_accessed=1024, transcendentals=0)


def work(flops):
    return pl.CostEstimate(flops=int(flops), bytes_accessed=1024, transcendentals=0)


def shaped(kind, *shape):
    return jax.ShapeDtypeStruct(shape, kind)


def prepare_body(spot, query_grads, mine, mine_stay, sending):
    rank = LANES // 2
    rows, width = query_grads.shape
    for outs, side in (((mine, mine_stay), spot[0]), ((sending,), 1 - spot[0])):
        for m in range(width // 4 // LANES):
            at = pl.multiple_of(side * (width // 4) + m * LANES, LANES)
            low = query_grads[:, pl.ds(at, LANES)]
            high = query_grads[:, pl.ds(at + width // 2, LANES)]
            even = jnp.concatenate([low[:, :rank], high[:, :rank]], 1)
            odd = jnp.concatenate([low[:, rank:], high[:, rank:]], 1)
            for out in outs:
                for k, block in ((2 * m, even), (2 * m + 1, odd)):
                    if k * LANES < out.shape[1]:
                        out[:, k * LANES:(k + 1) * LANES] = block


def prepare(query_grads, spot, stay):
    rows, width = query_grads.shape
    half = width // 2
    return pl.pallas_call(
        prepare_body,
        in_specs=[SCALARS, WHOLE],
        out_specs=[WHOLE] * 3,
        out_shape=[shaped(bf16, *size) for size in ((rows, half), (rows, stay), (rows, half))],
        compiler_params=LIMIT,
    )(spot, query_grads)


def form_body(rows, rank, spot, inputs, outgrads, mask, *refs):
    kept, lent, sent, sent_lent, rounds = refs[-5:]
    for d in range(rows):
        masked = outgrads[d] * mask[d:d + 1, :].astype(bf16)
        product = lax.dot_general(inputs[d], masked, NT, preferred_element_type=f32)
        pairs = jnp.concatenate([product[:rank // 2], product[rank // 2:]], 1)
        rounds[pl.ds(d, rank // 2, stride=rows), :] = pairs
    stay = sent.shape[1] // LANES
    for which in range(2):
        side = spot[0] if which == 0 else 1 - spot[0]
        for k in range(rank // 4):
            at = pl.multiple_of((side * (rank // 4) + k) * rows, rows)
            block = rounds[pl.ds(at, rows), :].astype(bf16)
            if which == 0:
                kept[:, k * LANES:(k + 1) * LANES] = block
                if k >= stay:
                    lent[:, (k - stay) * LANES:(k - stay + 1) * LANES] = block
            elif k < stay:
                sent[:, k * LANES:(k + 1) * LANES] = block
            else:
                sent_lent[:, (k - stay) * LANES:(k - stay + 1) * LANES] = block


def form(doc_inputs, doc_outgrads, token_mask, spot, stay, *after):
    docs, rank, length = doc_inputs.shape
    rows = 64
    steps = docs // rows
    half = rank * rank // 2
    widths = (half, half - stay, stay, half - stay)

    def at(g, spot):
        return lax.rem(g + spot[1] * (steps // 2), steps)

    return pl.pallas_call(
        functools.partial(form_body, rows, rank),
        grid_spec=pltpu.PrefetchScalarGridSpec(
            num_scalar_prefetch=1,
            grid=(steps,),
            in_specs=[
                pl.BlockSpec((rows, rank, length), lambda g, spot: (at(g, spot), 0, 0)),
                pl.BlockSpec((rows, rank, length), lambda g, spot: (at(g, spot), 0, 0)),
                pl.BlockSpec((rows, length), lambda g, spot: (at(g, spot), 0)),
            ] + [ANYWHERE] * len(after),
            out_specs=[pl.BlockSpec((rows, width), lambda g, spot: (g, 0)) for width in widths],
            scratch_shapes=[pltpu.VMEM((rank // 2 * rows, LANES), f32)],
        ),
        out_shape=[shaped(bf16, docs, width) for width in widths],
        compiler_params=LIMIT,
        cost_estimate=pl.CostEstimate(
            flops=40 * docs * rank * rank * length, bytes_accessed=4 * docs * rank * length + 2 * docs * rank * rank, transcendentals=0
        ),
    )(spot, doc_inputs, doc_outgrads, token_mask, *after)


def tie(arrays, *after):
    count = len(arrays)
    return pl.pallas_call(
        lambda *refs: None,
        in_specs=[ANYWHERE] * (count + len(after)),
        out_specs=[ANYWHERE] * count,
        out_shape=[shaped(a.dtype, *a.shape) for a in arrays],
        input_output_aliases={i: i for i in range(count)},
        compiler_params=LIMIT,
        cost_estimate=FREE,
    )(*arrays, *after)


def dot(rows, block):
    return lax.dot_general(rows, block, NT, preferred_element_type=f32)


def score_body(stay, counts, spot, own, far, far_lent, *refs):
    keep, give = refs[-2:]
    part = own.shape[0] // 2

    def put(block, at):
        width = block.shape[1]
        lent = block.shape[1] > stay

        def products(h):
            rows = slice(h * part, (h + 1) * part)
            reach = dot(far[rows, :], block[:, :stay])
            if lent:
                reach += dot(far_lent[rows, :], block[:, stay:])
            return dot(own[rows, :width], block[...]), reach

        keep[:part, at], keep[part:, at] = products(0)
        mate, opposite = products(1)
        give[:part, at] = mate.astype(bf16)
        give[part:, at] = opposite.astype(bf16)

    def group(blocks):
        for i, block in enumerate(blocks):
            size = block.shape[0]
            if len(blocks) == 1:
                at = slice(None)
            else:
                at = pl.ds(pl.multiple_of((spot[0] if i == 0 else 1 - spot[0]) * size, size), size)
            put(block, at)

    if counts[1]:
        pl.when(spot[2] == 1)(lambda: group(refs[:counts[0]]))
        pl.when(spot[2] == 0)(lambda: group(refs[counts[0]:sum(counts)]))
    else:
        group(refs[:counts[0]])


def score(spot, stay, docs, blocks, outer, *after):
    rows = docs[0].shape[0]
    queries = sum(block.shape[0] for block in blocks)
    return pl.pallas_call(
        functools.partial(score_body, stay, (len(blocks), len(outer))),
        in_specs=[SCALARS] + [WHOLE] * (3 + len(blocks) + len(outer)) + [ANYWHERE] * len(after),
        out_specs=[WHOLE] * 2,
        out_shape=[shaped(f32, rows, queries), shaped(bf16, rows, queries)],
        compiler_params=LIMIT,
        cost_estimate=work(5 * rows * 2 * queries * docs[0].shape[1]) if outer else FREE,
    )(spot, *docs, *blocks, *outer, *after)


def lent_body(stay, count, spot, near, far, *refs):
    keep, give = refs[-2:]
    part = near.shape[0] // 2

    @pl.when(spot[2] == 1)
    def _():
        for g in range(count // 2):
            blocks = refs[2 * g:2 * g + 2]
            rows = blocks[0].shape[0]
            for i, block in enumerate(blocks):
                size = block.shape[0]
                slot = 2 * g * rows + (spot[0] if i == 0 else 1 - spot[0]) * rows
                at = pl.ds(pl.multiple_of(slot, size), size)
                for r, docs in enumerate((near, far)):
                    rows_at = slice(r * part, (r + 1) * part)
                    keep[rows_at, at] = dot(docs[:part, :], block[:, stay:])
                    give[rows_at, at] = dot(docs[part:, :], block[:, stay:]).astype(bf16)


def lent_score(spot, stay, near, far, blocks, *after):
    docs = near.shape[0]
    queries = sum(block.shape[0] for block in blocks)
    return pl.pallas_call(
        functools.partial(lent_body, stay, len(blocks)),
        in_specs=[SCALARS] + [WHOLE] * (2 + len(blocks)) + [ANYWHERE] * len(after),
        out_specs=[WHOLE] * 2,
        out_shape=[shaped(f32, docs, queries), shaped(bf16, docs, queries)],
        compiler_params=LIMIT,
        cost_estimate=work(2.5 * 2 * docs * 2 * queries * near.shape[1]),
    )(spot, near, far, *blocks, *after)


def last_body(stay, spot, own, far, far_lent, inner, outer, *refs):
    near, mate, across, diagonal = refs[-4:]
    part = near.shape[0]

    def products(block):
        def reach(rows):
            return dot(far[rows, :], block[:, :stay]) + dot(far_lent[rows, :], block[:, stay:])

        mate[...] = dot(own[part:, :], block[...]).astype(bf16)
        across[...] = reach(slice(part)).astype(bf16)
        diagonal[...] = reach(slice(part, None)).astype(bf16)
        near[...] = dot(own[:part, :], block[...])

    pl.when(spot[2] == 1)(lambda: products(inner))
    pl.when(spot[2] == 0)(lambda: products(outer))


def last_score(spot, stay, docs, inner, outer, *after):
    shape = (docs[0].shape[0] // 2, inner.shape[0])
    return pl.pallas_call(
        functools.partial(last_body, stay),
        in_specs=[SCALARS] + [WHOLE] * 5 + [ANYWHERE] * len(after),
        out_specs=[WHOLE] * 4,
        out_shape=[shaped(f32, *shape)] + [shaped(bf16, *shape)] * 3,
        compiler_params=LIMIT,
        cost_estimate=work(2 * 2 * docs[0].shape[0] * 2 * inner.shape[0] * inner.shape[1]),
    )(spot, *docs, inner, outer, *after)


def on_device(doc_inputs, doc_outgrads, token_mask, query_grads):
    blk = lax.axis_size("blk")
    places = blk // 2
    me = lax.axis_index("blk")
    place, side = me // 2, me % 2
    docs, rank = doc_inputs.shape[0], doc_inputs.shape[2]
    queries = query_grads.shape[0]
    part = docs // 2
    half = rank * rank // 2
    doc_inputs = doc_inputs.reshape(docs, *doc_inputs.shape[2:])
    doc_outgrads = doc_outgrads.reshape(docs, *doc_outgrads.shape[2:])
    lending = places == 4
    stay = half // 16 * (16 - LENT)
    inner = jnp.where((place == 1) | (place == 2), 1, 0) if lending else 1
    spot = jnp.stack([side, lax.axis_index("proj"), inner]).astype(jnp.int32)

    def at(place):
        return [2 * place, 2 * place + 1]

    across = [(b, b ^ 1) for b in range(blk)]
    onward = [(b, (b + 2) % blk) for b in range(blk)]
    inward = list(zip(at(0) + at(3), at(1) + at(2)))
    outward = [(b, a) for a, b in inward]
    centre = list(zip(at(1) + at(2), at(2) + at(1)))
    inner_across = [(b, b ^ 1) for b in at(1) + at(2)]
    inner_cores = [(2 * b + c, 2 * b + 1 - c) for b in at(1) + at(2) for c in range(2)]
    diagonal = [(2 * b + c, 2 * (b ^ 1) + (c ^ 1)) for b in range(blk) for c in range(2)]

    def move(x, pairs):
        return lax.ppermute(x, "blk", pairs)

    def swap_across(x):
        return move(x, across)

    def swap_cores(x):
        return lax.ppermute(x, "proj", [(0, 1), (1, 0)])

    def swap_diagonal(x):
        return lax.ppermute(x, ("blk", "proj"), diagonal)

    def over_cores(keep, give, swap=swap_cores):
        got = swap(give).astype(f32)
        return keep[:part] + got[:part], (keep[part:] + got[part:]).astype(bf16)

    out = jnp.zeros((part, blk * queries), f32)

    def put(out, total, origin, at):
        return lax.dynamic_update_slice_in_dim(out, total, origin * (2 * queries) + at, 1)

    mine, mine_stay, sending = prepare(query_grads, spot, stay)

    if not lending:
        flow = [mine, swap_across(sending)]
        own, _, sent, sent_lent = form(doc_inputs, doc_outgrads, token_mask, spot, stay)
        rows = own, swap_across(sent), swap_across(sent_lent)
        for step in range(places):
            keep, give = score(spot, stay, rows, flow, [])
            total, reach = over_cores(keep, give)
            out = put(out, total + swap_across(reach).astype(f32), (place - step + places) % places, 0)
            if step + 1 < places:
                flow = [move(x, onward) for x in flow]
        return out

    def staying(*blocks):
        return jnp.concatenate([x[:, :stay] for x in blocks], 0)

    mate_a = move(mine, inward)
    near_a = move(mine, centre)
    outer_mate_a = move(mine_stay, outward)
    other = swap_across(sending)
    own, lent, sent, sent_lent = form(doc_inputs, doc_outgrads, token_mask, spot, stay)
    sent, sent_lent, mate_a, near_a, other = tie((sent, sent_lent, mate_a, near_a, other), outer_mate_a)

    outer_mate_b = move(other[:, :stay], outward)
    outer_near_a = move(near_a[:, :stay], outward)
    away_a = move(mate_a, centre)
    mate_b = move(other, inward)
    far = swap_across(sent)
    lent, sent_lent, away_a, other, mate_b = tie(
        (lent, sent_lent, away_a, other, mate_b), outer_mate_b, outer_near_a, far
    )

    outer_away_a = move(away_a, outward)
    near_b = move(other, centre)
    lent_near = move(lent, inward)
    far_lent = swap_across(sent_lent)
    lent_far = move(far_lent, inward)
    outer_near_b = move(near_b[:, :stay], outward)
    away_b = [move(x, centre) for x in jnp.split(mate_b, 2, 0)]
    outer_away_b = [move(x, outward) for x in away_b]

    rows = own, far, far_lent
    origins = {"self": place, "mate": place ^ 1, "near": jnp.where(place < 2, 2, 1), "away": jnp.where(place < 2, 3, 0)}

    keep, give = score(spot, stay, rows, [mine, other], [], near_b, outer_away_a, lent_near)
    self_total, self_reach = over_cores(keep, give)
    self_beside = swap_across(self_reach)
    keep, give = score(spot, stay, rows, [mate_a, mate_b], [outer_mate_a, outer_mate_b], give, outer_near_b, lent_far, away_b[0])
    mate_total, mate_reach = over_cores(keep, give)
    mate_beside = swap_across(mate_reach)
    keep, give = lent_score(spot, stay, lent_near, lent_far, [mine, other, near_a, near_b], give, self_reach)
    lent_total, lent_reach = over_cores(keep, give, lambda x: lax.ppermute(x, ("blk", "proj"), inner_cores))
    lent_beside = move(lent_reach, inner_across)
    returned = move((lent_total + lent_beside.astype(f32)).astype(bf16), outward).astype(f32)
    keep, give = score(
        spot, stay, rows, [near_a, near_b], [outer_near_a, outer_near_b], give, mate_reach, lent_reach, outer_away_b[0], away_b[1]
    )
    near_total, near_reach = over_cores(keep, give)
    near_beside = swap_across(near_reach)
    keep, give = score(spot, stay, rows, [away_a], [outer_away_a], give)
    away_total, reach = over_cores(keep, give)
    away_beside = swap_across(reach)
    out = put(out, self_total + self_beside.astype(f32), origins["self"], 0)

    size = queries // 2
    last = (give, lent_beside, self_beside)
    for i in range(2):
        near, give, facing, opposite = last_score(spot, stay, rows, away_b[i], outer_away_b[i], *last)
        cut = slice(i * size, (i + 1) * size)
        mine_total = away_total[:, cut] + swap_across(facing).astype(f32) + swap_diagonal(opposite).astype(f32)
        other_total = near + swap_cores(give).astype(f32) + away_beside[:, cut].astype(f32)
        out = put(out, mine_total, origins["away"], side * queries + i * size)
        out = put(out, other_total, origins["away"], (1 - side) * queries + i * size)
        last = (near,)

    out = put(out, mate_total + mate_beside.astype(f32) + returned[:, :2 * queries], origins["mate"], 0)
    out = put(out, near_total + near_beside.astype(f32) + returned[:, 2 * queries:], origins["near"], 0)
    return out


def solution(mesh):
    placed = (
        P(("grp", "blk"), "proj", None, None),
        P(("grp", "blk"), "proj", None, None),
        P(("grp", "blk"), None),
        P(("grp", "blk"), "proj"),
    )
    return jax.shard_map(
        on_device,
        mesh=mesh,
        in_specs=placed,
        out_specs=P(("grp", "blk", "proj"), None),
        check_vma=False,
    )
```

```python
import functools

import jax
import jax.numpy as jnp
from jax import lax
from jax.experimental import pallas as pl
from jax.experimental.pallas import tpu as pltpu
from jax.sharding import PartitionSpec as P

LANES = 128
VMEM_LIMIT = 48 * 1024 * 1024
ANYWHERE = pl.BlockSpec(memory_space=pl.ANY)
SCALARS = pl.BlockSpec(memory_space=pltpu.SMEM)
WHOLE = pl.BlockSpec(memory_space=pltpu.VMEM)
NT = (((1,), (1,)), ((), ()))
bf16, f32 = jnp.bfloat16, jnp.float32
LIMIT = pltpu.CompilerParams(vmem_limit_bytes=VMEM_LIMIT)


def shaped(kind, *shape):
    return jax.ShapeDtypeStruct(shape, kind)


def prepare_body(spot, low, high, *outs):
    rank = LANES // 2
    for m in range(low.shape[1] // LANES):
        at = slice(m * LANES, (m + 1) * LANES)
        even = jnp.concatenate([low[:, at][:, :rank], high[:, at][:, :rank]], 1)
        odd = jnp.concatenate([low[:, at][:, rank:], high[:, at][:, rank:]], 1)
        for i, out in enumerate(outs):
            cut = slice(i * out.shape[0], (i + 1) * out.shape[0])
            out[:, 2 * m * LANES:(2 * m + 1) * LANES] = even[cut, :]
            out[:, (2 * m + 1) * LANES:(2 * m + 2) * LANES] = odd[cut, :]


def prepare(query_grads, side, parts):
    rows, width = query_grads.shape
    steps = 2
    take = width // 4 // steps
    return pl.pallas_call(
        prepare_body,
        grid_spec=pltpu.PrefetchScalarGridSpec(
            num_scalar_prefetch=1,
            grid=(steps,),
            in_specs=[
                pl.BlockSpec((rows, take), lambda g, spot: (0, spot[0] * steps + g)),
                pl.BlockSpec((rows, take), lambda g, spot: (0, (2 + spot[0]) * steps + g)),
            ],
            out_specs=[pl.BlockSpec((rows // parts, 2 * take), lambda g, spot: (0, g))] * parts,
        ),
        out_shape=[shaped(bf16, rows // parts, width // 2)] * parts,
        compiler_params=LIMIT,
    )(side.astype(jnp.int32).reshape(1), query_grads, query_grads)


def form_body(rows, rank, spot, inputs, outgrads, mask, kept, sent, rounds):
    for d in range(rows):
        masked = outgrads[d] * mask[d:d + 1, :].astype(bf16)
        product = lax.dot_general(inputs[d], masked, NT, preferred_element_type=f32)
        pairs = jnp.concatenate([product[:rank // 2], product[rank // 2:]], 1)
        rounds[pl.ds(d, rank // 2, stride=rows), :] = pairs
    for out, side in ((kept, spot[0]), (sent, 1 - spot[0])):
        for k in range(rank // 4):
            at = pl.multiple_of((side * (rank // 4) + k) * rows, rows)
            out[:, k * LANES:(k + 1) * LANES] = rounds[pl.ds(at, rows), :].astype(bf16)


def form(doc_inputs, doc_outgrads, token_mask, spot):
    docs, rank, length = doc_inputs.shape
    rows = 64
    steps = docs // rows
    half = rank * rank // 2

    def at(g, spot):
        return lax.rem(g + spot[1] * (steps // 2), steps)

    return pl.pallas_call(
        functools.partial(form_body, rows, rank),
        grid_spec=pltpu.PrefetchScalarGridSpec(
            num_scalar_prefetch=1,
            grid=(steps,),
            in_specs=[
                pl.BlockSpec((rows, rank, length), lambda g, spot: (at(g, spot), 0, 0)),
                pl.BlockSpec((rows, rank, length), lambda g, spot: (at(g, spot), 0, 0)),
                pl.BlockSpec((rows, length), lambda g, spot: (at(g, spot), 0)),
            ],
            out_specs=[pl.BlockSpec((rows, half), lambda g, spot: (g, 0))] * 2,
            scratch_shapes=[pltpu.VMEM((rank // 2 * rows, LANES), f32)],
        ),
        out_shape=[shaped(bf16, docs, half)] * 2,
        compiler_params=LIMIT,
        cost_estimate=pl.CostEstimate(
            flops=40 * docs * rank * rank * length, bytes_accessed=4 * docs * rank * length + 2 * docs * rank * rank, transcendentals=0
        ),
    )(spot, doc_inputs, doc_outgrads, token_mask)


def tie(arrays, *after):
    count = len(arrays)
    return pl.pallas_call(
        lambda *refs: None,
        in_specs=[ANYWHERE] * (count + len(after)),
        out_specs=[ANYWHERE] * count,
        out_shape=[shaped(a.dtype, *a.shape) for a in arrays],
        input_output_aliases={i: i for i in range(count)},
        compiler_params=LIMIT,
    )(*arrays, *after)


def dot(rows, block):
    return lax.dot_general(rows, block, NT, preferred_element_type=f32)


FREE = pl.CostEstimate(flops=1024, bytes_accessed=1024, transcendentals=0)


def score_body(count, spot, own, far, *refs):
    keep, give = refs[-2:]
    part = own.shape[0] // 2
    for i, block in enumerate(refs[:count]):
        size = block.shape[0]
        if count == 3:
            rows = refs[0].shape[0]
            at = spot[0] * rows if i == 0 else (1 - spot[0]) * rows + (i - 1) * size
            columns = pl.ds(pl.multiple_of(at, size), size)
        else:
            columns = pl.ds(i * size, size)
        keep[:part, columns] = dot(own[:part, :], block[...])
        keep[part:, columns] = dot(far[:part, :], block[...])
        give[:part, columns] = dot(own[part:, :], block[...]).astype(bf16)
        give[part:, columns] = dot(far[part:, :], block[...]).astype(bf16)


def score(spot, own, far, blocks, *after):
    docs = own.shape[0]
    count = len(blocks)
    queries = sum(block.shape[0] for block in blocks)
    return pl.pallas_call(
        functools.partial(score_body, count),
        in_specs=[SCALARS] + [WHOLE] * (2 + count) + [ANYWHERE] * len(after),
        out_specs=[WHOLE] * 2,
        out_shape=[shaped(f32, docs, queries), shaped(bf16, docs, queries)],
        compiler_params=LIMIT,
        cost_estimate=FREE,
    )(spot, own, far, *blocks, *after)


def last_body(own, far, block, *refs):
    near, mate, across, diagonal = refs[-4:]
    part = near.shape[0]
    mate[...] = dot(own[part:, :], block[...]).astype(bf16)
    across[...] = dot(far[:part, :], block[...]).astype(bf16)
    diagonal[...] = dot(far[part:, :], block[...]).astype(bf16)
    near[...] = dot(own[:part, :], block[...])


def last_score(own, far, block, *after):
    shape = (own.shape[0] // 2, block.shape[0])
    return pl.pallas_call(
        last_body,
        in_specs=[WHOLE] * 3 + [ANYWHERE] * len(after),
        out_specs=[WHOLE] * 4,
        out_shape=[shaped(f32, *shape)] + [shaped(bf16, *shape)] * 3,
        compiler_params=LIMIT,
        cost_estimate=FREE,
    )(own, far, block, *after)


def on_device(doc_inputs, doc_outgrads, token_mask, query_grads):
    blk = lax.axis_size("blk")
    places = blk // 2
    me = lax.axis_index("blk")
    place, side = me // 2, me % 2
    spot = jnp.stack([side, lax.axis_index("proj")]).astype(jnp.int32)
    docs = doc_inputs.shape[0]
    queries = query_grads.shape[0]
    part = docs // 2

    across = [(b, b ^ 1) for b in range(blk)]
    onward = [(b, (b + 2) % blk) for b in range(blk)]
    diagonal = [(2 * b + c, 2 * (b ^ 1) + (c ^ 1)) for b in range(blk) for c in range(2)]

    def swap_across(x):
        return lax.ppermute(x, "blk", across)

    def swap_cores(x):
        return lax.ppermute(x, "proj", [(0, 1), (1, 0)])

    def pass_on(x):
        return lax.ppermute(x, "blk", onward)

    def swap_diagonal(x):
        return lax.ppermute(x, ("blk", "proj"), diagonal)

    (mine,) = prepare(query_grads, side, 1)
    ahead = pass_on(mine)
    sending = prepare(query_grads, 1 - side, 2)
    other = [swap_across(x) for x in sending]
    own, sent = form(
        doc_inputs.reshape(docs, *doc_inputs.shape[2:]), doc_outgrads.reshape(docs, *doc_outgrads.shape[2:]), token_mask, spot
    )
    sent, ahead, *other = tie((sent, ahead, *other))
    far = swap_across(sent)
    first, second = [mine, ahead], [other]
    for step in range(2, places):
        first.append(pass_on(first[-1]))
    for step in range(1, places):
        second.append([pass_on(x) for x in second[-1]])
    pieces = second[-1]

    out = jnp.zeros((part, blk * queries), f32)

    def put(out, total, step, at):
        origin = (place - step + places) % places
        return lax.dynamic_update_slice_in_dim(out, total, origin * (2 * queries) + at, 1)

    def over_cores(keep, give):
        got = swap_cores(give).astype(f32)
        return keep[:part] + got[:part], (keep[part:] + got[part:]).astype(bf16)

    besides = []
    last = (first[2], second[1][0]) if places > 2 else ()
    for step in range(places - 2):
        keep, give = score(spot, own, far, [first[step]] + second[step], *last)
        total, reach = over_cores(keep, give)
        besides.append(swap_across(reach))
        out = put(out, total + besides[-1].astype(f32), step, 0)
        last = (give,)

    keep, give = score(spot, own, far, first[-2:], *last)
    early, early_reach = over_cores(keep, give)
    early_beside = swap_across(early_reach)
    keep, give = score(spot, own, far, second[-2], give, *besides)
    late, late_reach = over_cores(keep, give)
    late_beside = swap_across(late_reach)
    out = put(out, early[:, :queries] + late_beside.astype(f32), places - 2, side * queries)
    out = put(out, late + early_beside[:, :queries].astype(f32), places - 2, (1 - side) * queries)

    size = queries // 2
    last = (give, early_beside)
    for i, piece in enumerate(pieces):
        near, give, facing, opposite = last_score(own, far, piece, *last)
        cut = slice(queries + i * size, queries + (i + 1) * size)
        mine_total = early[:, cut] + swap_across(facing).astype(f32) + swap_diagonal(opposite).astype(f32)
        other_total = near + swap_cores(give).astype(f32) + early_beside[:, cut].astype(f32)
        out = put(out, mine_total, places - 1, side * queries + i * size)
        out = put(out, other_total, places - 1, (1 - side) * queries + i * size)
        last = (near, late_reach)
    return out


def solution(mesh):
    placed = (
        P(("grp", "blk"), "proj", None, None),
        P(("grp", "blk"), "proj", None, None),
        P(("grp", "blk"), None),
        P(("grp", "blk"), "proj"),
    )
    return jax.shard_map(
        on_device,
        mesh=mesh,
        in_specs=placed,
        out_specs=P(("grp", "blk", "proj"), None),
        check_vma=False,
    )
```

```python
import functools

import jax
import jax.numpy as jnp
from jax import lax
from jax.experimental import pallas as pl
from jax.experimental.pallas import tpu as pltpu
from jax.sharding import PartitionSpec as P

LANES = 128
VMEM_LIMIT = 48 * 1024 * 1024
ANYWHERE = pl.BlockSpec(memory_space=pl.ANY)
SCALARS = pl.BlockSpec(memory_space=pltpu.SMEM)
WHOLE = pl.BlockSpec(memory_space=pltpu.VMEM)
NT = (((1,), (1,)), ((), ()))
bf16, f32 = jnp.bfloat16, jnp.float32
LIMIT = pltpu.CompilerParams(vmem_limit_bytes=VMEM_LIMIT)


def shaped(kind, *shape):
    return jax.ShapeDtypeStruct(shape, kind)


def prepare_body(spot, query_grads, mine, *sending):
    rank = LANES // 2
    rows, width = query_grads.shape
    for outs, side in (((mine,), spot[0]), (sending, 1 - spot[0])):
        for m in range(width // 4 // LANES):
            at = pl.multiple_of(side * (width // 4) + m * LANES, LANES)
            low = query_grads[:, pl.ds(at, LANES)]
            high = query_grads[:, pl.ds(at + width // 2, LANES)]
            even = jnp.concatenate([low[:, :rank], high[:, :rank]], 1)
            odd = jnp.concatenate([low[:, rank:], high[:, rank:]], 1)
            for i, out in enumerate(outs):
                cut = slice(i * out.shape[0], (i + 1) * out.shape[0])
                out[:, 2 * m * LANES:(2 * m + 1) * LANES] = even[cut, :]
                out[:, (2 * m + 1) * LANES:(2 * m + 2) * LANES] = odd[cut, :]


def prepare(query_grads, spot):
    rows, width = query_grads.shape
    return pl.pallas_call(
        prepare_body,
        in_specs=[SCALARS, WHOLE],
        out_specs=[WHOLE] * 3,
        out_shape=[shaped(bf16, size, width // 2) for size in (rows, rows // 2, rows // 2)],
        compiler_params=LIMIT,
    )(spot, query_grads)


def form_body(rows, rank, spot, inputs, outgrads, mask, kept, sent, rounds):
    for d in range(rows):
        masked = outgrads[d] * mask[d:d + 1, :].astype(bf16)
        product = lax.dot_general(inputs[d], masked, NT, preferred_element_type=f32)
        pairs = jnp.concatenate([product[:rank // 2], product[rank // 2:]], 1)
        rounds[pl.ds(d, rank // 2, stride=rows), :] = pairs
    for out, side in ((kept, spot[0]), (sent, 1 - spot[0])):
        for k in range(rank // 4):
            at = pl.multiple_of((side * (rank // 4) + k) * rows, rows)
            out[:, k * LANES:(k + 1) * LANES] = rounds[pl.ds(at, rows), :].astype(bf16)


def form(doc_inputs, doc_outgrads, token_mask, spot):
    docs, rank, length = doc_inputs.shape
    rows = 64
    steps = docs // rows
    half = rank * rank // 2

    def at(g, spot):
        return lax.rem(g + spot[1] * (steps // 2), steps)

    return pl.pallas_call(
        functools.partial(form_body, rows, rank),
        grid_spec=pltpu.PrefetchScalarGridSpec(
            num_scalar_prefetch=1,
            grid=(steps,),
            in_specs=[
                pl.BlockSpec((rows, rank, length), lambda g, spot: (at(g, spot), 0, 0)),
                pl.BlockSpec((rows, rank, length), lambda g, spot: (at(g, spot), 0, 0)),
                pl.BlockSpec((rows, length), lambda g, spot: (at(g, spot), 0)),
            ],
            out_specs=[pl.BlockSpec((rows, half), lambda g, spot: (g, 0))] * 2,
            scratch_shapes=[pltpu.VMEM((rank // 2 * rows, LANES), f32)],
        ),
        out_shape=[shaped(bf16, docs, half)] * 2,
        compiler_params=LIMIT,
        cost_estimate=pl.CostEstimate(
            flops=40 * docs * rank * rank * length, bytes_accessed=4 * docs * rank * length + 2 * docs * rank * rank, transcendentals=0
        ),
    )(spot, doc_inputs, doc_outgrads, token_mask)


def tie(arrays, *after):
    count = len(arrays)
    return pl.pallas_call(
        lambda *refs: None,
        in_specs=[ANYWHERE] * (count + len(after)),
        out_specs=[ANYWHERE] * count,
        out_shape=[shaped(a.dtype, *a.shape) for a in arrays],
        input_output_aliases={i: i for i in range(count)},
        compiler_params=LIMIT,
    )(*arrays, *after)


def dot(rows, block):
    return lax.dot_general(rows, block, NT, preferred_element_type=f32)


FREE = pl.CostEstimate(flops=1024, bytes_accessed=1024, transcendentals=0)


def score_body(count, spot, own, far, *refs):
    keep, give = refs[-2:]
    part = own.shape[0] // 2
    for i, block in enumerate(refs[:count]):
        size = block.shape[0]
        if count == 3:
            rows = refs[0].shape[0]
            at = spot[0] * rows if i == 0 else (1 - spot[0]) * rows + (i - 1) * size
            columns = pl.ds(pl.multiple_of(at, size), size)
        else:
            columns = pl.ds(i * size, size)
        keep[:part, columns] = dot(own[:part, :], block[...])
        keep[part:, columns] = dot(far[:part, :], block[...])
        give[:part, columns] = dot(own[part:, :], block[...]).astype(bf16)
        give[part:, columns] = dot(far[part:, :], block[...]).astype(bf16)


def score(spot, own, far, blocks, *after):
    docs = own.shape[0]
    count = len(blocks)
    queries = sum(block.shape[0] for block in blocks)
    return pl.pallas_call(
        functools.partial(score_body, count),
        in_specs=[SCALARS] + [WHOLE] * (2 + count) + [ANYWHERE] * len(after),
        out_specs=[WHOLE] * 2,
        out_shape=[shaped(f32, docs, queries), shaped(bf16, docs, queries)],
        compiler_params=LIMIT,
        cost_estimate=FREE,
    )(spot, own, far, *blocks, *after)


def last_body(own, far, block, *refs):
    near, mate, across, diagonal = refs[-4:]
    part = near.shape[0]
    mate[...] = dot(own[part:, :], block[...]).astype(bf16)
    across[...] = dot(far[:part, :], block[...]).astype(bf16)
    diagonal[...] = dot(far[part:, :], block[...]).astype(bf16)
    near[...] = dot(own[:part, :], block[...])


def last_score(own, far, block, *after):
    shape = (own.shape[0] // 2, block.shape[0])
    return pl.pallas_call(
        last_body,
        in_specs=[WHOLE] * 3 + [ANYWHERE] * len(after),
        out_specs=[WHOLE] * 4,
        out_shape=[shaped(f32, *shape)] + [shaped(bf16, *shape)] * 3,
        compiler_params=LIMIT,
        cost_estimate=FREE,
    )(own, far, block, *after)


def on_device(doc_inputs, doc_outgrads, token_mask, query_grads):
    blk = lax.axis_size("blk")
    places = blk // 2
    me = lax.axis_index("blk")
    place, side = me // 2, me % 2
    spot = jnp.stack([side, lax.axis_index("proj")]).astype(jnp.int32)
    docs = doc_inputs.shape[0]
    queries = query_grads.shape[0]
    part = docs // 2

    across = [(b, b ^ 1) for b in range(blk)]
    onward = [(b, (b + 2) % blk) for b in range(blk)]
    diagonal = [(2 * b + c, 2 * (b ^ 1) + (c ^ 1)) for b in range(blk) for c in range(2)]

    def swap_across(x):
        return lax.ppermute(x, "blk", across)

    def swap_cores(x):
        return lax.ppermute(x, "proj", [(0, 1), (1, 0)])

    def pass_on(x):
        return lax.ppermute(x, "blk", onward)

    def swap_diagonal(x):
        return lax.ppermute(x, ("blk", "proj"), diagonal)

    mine, *sending = prepare(query_grads, spot)
    ahead = pass_on(mine)
    other = [swap_across(x) for x in sending]
    own, sent = form(
        doc_inputs.reshape(docs, *doc_inputs.shape[2:]), doc_outgrads.reshape(docs, *doc_outgrads.shape[2:]), token_mask, spot
    )
    sent, ahead, *other = tie((sent, ahead, *other))
    far = swap_across(sent)
    first, second = [mine, ahead], [other]
    for step in range(2, places):
        first.append(pass_on(first[-1]))
    for step in range(1, places):
        second.append([pass_on(x) for x in second[-1]])
    pieces = second[-1]

    out = jnp.zeros((part, blk * queries), f32)

    def put(out, total, step, at):
        origin = (place - step + places) % places
        return lax.dynamic_update_slice_in_dim(out, total, origin * (2 * queries) + at, 1)

    def over_cores(keep, give):
        got = swap_cores(give).astype(f32)
        return keep[:part] + got[:part], (keep[part:] + got[part:]).astype(bf16)

    besides = []
    last = (first[2], second[1][0]) if places > 2 else ()
    for step in range(places - 2):
        keep, give = score(spot, own, far, [first[step]] + second[step], *last)
        total, reach = over_cores(keep, give)
        besides.append(swap_across(reach))
        out = put(out, total + besides[-1].astype(f32), step, 0)
        last = (give,)

    keep, give = score(spot, own, far, first[-2:], *last)
    early, early_reach = over_cores(keep, give)
    early_beside = swap_across(early_reach)
    keep, give = score(spot, own, far, second[-2], give, besides[0])
    late, late_reach = over_cores(keep, give)
    late_beside = swap_across(late_reach)
    out = put(out, early[:, :queries] + late_beside.astype(f32), places - 2, side * queries)
    out = put(out, late + early_beside[:, :queries].astype(f32), places - 2, (1 - side) * queries)

    size = queries // 2
    last = (give, early_reach)
    for i, piece in enumerate(pieces):
        near, give, facing, opposite = last_score(own, far, piece, *last)
        cut = slice(queries + i * size, queries + (i + 1) * size)
        mine_total = early[:, cut] + swap_across(facing).astype(f32) + swap_diagonal(opposite).astype(f32)
        other_total = near + swap_cores(give).astype(f32) + early_beside[:, cut].astype(f32)
        out = put(out, mine_total, places - 1, side * queries + i * size)
        out = put(out, other_total, places - 1, (1 - side) * queries + i * size)
        last = (near, early_beside, late_reach)
    return out


def solution(mesh):
    placed = (
        P(("grp", "blk"), "proj", None, None),
        P(("grp", "blk"), "proj", None, None),
        P(("grp", "blk"), None),
        P(("grp", "blk"), "proj"),
    )
    return jax.shard_map(
        on_device,
        mesh=mesh,
        in_specs=placed,
        out_specs=P(("grp", "blk", "proj"), None),
        check_vma=False,
    )
```

```python
import functools

import jax
import jax.numpy as jnp
from jax import lax
from jax.experimental import pallas as pl
from jax.experimental.pallas import tpu as pltpu
from jax.sharding import PartitionSpec as P

LANES = 128
VMEM_LIMIT = 48 * 1024 * 1024
ANYWHERE = pl.BlockSpec(memory_space=pl.ANY)
SCALARS = pl.BlockSpec(memory_space=pltpu.SMEM)
WHOLE = pl.BlockSpec(memory_space=pltpu.VMEM)
NT = (((1,), (1,)), ((), ()))
bf16, f32 = jnp.bfloat16, jnp.float32
LIMIT = pltpu.CompilerParams(vmem_limit_bytes=VMEM_LIMIT)


def shaped(kind, *shape):
    return jax.ShapeDtypeStruct(shape, kind)


def prepare_body(spot, query_grads, mine, *sending):
    rank = LANES // 2
    rows, width = query_grads.shape
    for outs, side in (((mine,), spot[0]), (sending, 1 - spot[0])):
        for m in range(width // 4 // LANES):
            at = pl.multiple_of(side * (width // 4) + m * LANES, LANES)
            low = query_grads[:, pl.ds(at, LANES)]
            high = query_grads[:, pl.ds(at + width // 2, LANES)]
            even = jnp.concatenate([low[:, :rank], high[:, :rank]], 1)
            odd = jnp.concatenate([low[:, rank:], high[:, rank:]], 1)
            for i, out in enumerate(outs):
                cut = slice(i * out.shape[0], (i + 1) * out.shape[0])
                out[:, 2 * m * LANES:(2 * m + 1) * LANES] = even[cut, :]
                out[:, (2 * m + 1) * LANES:(2 * m + 2) * LANES] = odd[cut, :]


def prepare(query_grads, spot):
    rows, width = query_grads.shape
    return pl.pallas_call(
        prepare_body,
        in_specs=[SCALARS, WHOLE],
        out_specs=[WHOLE] * 3,
        out_shape=[shaped(bf16, size, width // 2) for size in (rows, rows // 2, rows // 2)],
        compiler_params=LIMIT,
    )(spot, query_grads)


def form_body(rows, rank, spot, inputs, outgrads, mask, kept, sent, rounds):
    for d in range(rows):
        masked = outgrads[d] * mask[d:d + 1, :].astype(bf16)
        product = lax.dot_general(inputs[d], masked, NT, preferred_element_type=f32)
        pairs = jnp.concatenate([product[:rank // 2], product[rank // 2:]], 1)
        rounds[pl.ds(d, rank // 2, stride=rows), :] = pairs
    for out, side in ((kept, spot[0]), (sent, 1 - spot[0])):
        for k in range(rank // 4):
            at = pl.multiple_of((side * (rank // 4) + k) * rows, rows)
            out[:, k * LANES:(k + 1) * LANES] = rounds[pl.ds(at, rows), :].astype(bf16)


def form(doc_inputs, doc_outgrads, token_mask, spot):
    docs, rank, length = doc_inputs.shape
    rows = 64
    steps = docs // rows
    half = rank * rank // 2

    def at(g, spot):
        return lax.rem(g + spot[1] * (steps // 2), steps)

    return pl.pallas_call(
        functools.partial(form_body, rows, rank),
        grid_spec=pltpu.PrefetchScalarGridSpec(
            num_scalar_prefetch=1,
            grid=(steps,),
            in_specs=[
                pl.BlockSpec((rows, rank, length), lambda g, spot: (at(g, spot), 0, 0)),
                pl.BlockSpec((rows, rank, length), lambda g, spot: (at(g, spot), 0, 0)),
                pl.BlockSpec((rows, length), lambda g, spot: (at(g, spot), 0)),
            ],
            out_specs=[pl.BlockSpec((rows, half), lambda g, spot: (g, 0))] * 2,
            scratch_shapes=[pltpu.VMEM((rank // 2 * rows, LANES), f32)],
        ),
        out_shape=[shaped(bf16, docs, half)] * 2,
        compiler_params=LIMIT,
        cost_estimate=pl.CostEstimate(
            flops=40 * docs * rank * rank * length, bytes_accessed=4 * docs * rank * length + 2 * docs * rank * rank, transcendentals=0
        ),
    )(spot, doc_inputs, doc_outgrads, token_mask)


def tie(arrays, *after):
    count = len(arrays)
    return pl.pallas_call(
        lambda *refs: None,
        in_specs=[ANYWHERE] * (count + len(after)),
        out_specs=[ANYWHERE] * count,
        out_shape=[shaped(a.dtype, *a.shape) for a in arrays],
        input_output_aliases={i: i for i in range(count)},
        compiler_params=LIMIT,
    )(*arrays, *after)


def dot(rows, block):
    return lax.dot_general(rows, block, NT, preferred_element_type=f32)


FREE = pl.CostEstimate(flops=1024, bytes_accessed=1024, transcendentals=0)


def score_body(count, spot, own, far, *refs):
    keep, give = refs[-2:]
    part = own.shape[0] // 2
    for i, block in enumerate(refs[:count]):
        size = block.shape[0]
        if count == 3:
            rows = refs[0].shape[0]
            at = spot[0] * rows if i == 0 else (1 - spot[0]) * rows + (i - 1) * size
            columns = pl.ds(pl.multiple_of(at, size), size)
        else:
            columns = pl.ds(i * size, size)
        keep[:part, columns] = dot(own[:part, :], block[...])
        keep[part:, columns] = dot(far[:part, :], block[...])
        give[:part, columns] = dot(own[part:, :], block[...]).astype(bf16)
        give[part:, columns] = dot(far[part:, :], block[...]).astype(bf16)


def score(spot, own, far, blocks, *after):
    docs = own.shape[0]
    count = len(blocks)
    queries = sum(block.shape[0] for block in blocks)
    return pl.pallas_call(
        functools.partial(score_body, count),
        in_specs=[SCALARS] + [WHOLE] * (2 + count) + [ANYWHERE] * len(after),
        out_specs=[WHOLE] * 2,
        out_shape=[shaped(f32, docs, queries), shaped(bf16, docs, queries)],
        compiler_params=LIMIT,
        cost_estimate=FREE,
    )(spot, own, far, *blocks, *after)


def last_body(own, far, block, *refs):
    near, mate, across, diagonal = refs[-4:]
    part = near.shape[0]
    mate[...] = dot(own[part:, :], block[...]).astype(bf16)
    across[...] = dot(far[:part, :], block[...]).astype(bf16)
    diagonal[...] = dot(far[part:, :], block[...]).astype(bf16)
    near[...] = dot(own[:part, :], block[...])


def last_score(own, far, block, *after):
    shape = (own.shape[0] // 2, block.shape[0])
    return pl.pallas_call(
        last_body,
        in_specs=[WHOLE] * 3 + [ANYWHERE] * len(after),
        out_specs=[WHOLE] * 4,
        out_shape=[shaped(f32, *shape)] + [shaped(bf16, *shape)] * 3,
        compiler_params=LIMIT,
        cost_estimate=FREE,
    )(own, far, block, *after)


def on_device(doc_inputs, doc_outgrads, token_mask, query_grads):
    blk = lax.axis_size("blk")
    places = blk // 2
    me = lax.axis_index("blk")
    place, side = me // 2, me % 2
    spot = jnp.stack([side, lax.axis_index("proj")]).astype(jnp.int32)
    docs = doc_inputs.shape[0]
    queries = query_grads.shape[0]
    part = docs // 2

    across = [(b, b ^ 1) for b in range(blk)]
    onward = [(b, (b + 2) % blk) for b in range(blk)]
    diagonal = [(2 * b + c, 2 * (b ^ 1) + (c ^ 1)) for b in range(blk) for c in range(2)]

    def swap_across(x):
        return lax.ppermute(x, "blk", across)

    def swap_cores(x):
        return lax.ppermute(x, "proj", [(0, 1), (1, 0)])

    def pass_on(x):
        return lax.ppermute(x, "blk", onward)

    def swap_diagonal(x):
        return lax.ppermute(x, ("blk", "proj"), diagonal)

    mine, *sending = prepare(query_grads, spot)
    ahead = pass_on(mine)
    other = [swap_across(x) for x in sending]
    own, sent = form(
        doc_inputs.reshape(docs, *doc_inputs.shape[2:]), doc_outgrads.reshape(docs, *doc_outgrads.shape[2:]), token_mask, spot
    )
    sent, ahead, *other = tie((sent, ahead, *other))
    far = swap_across(sent)
    first, second = [mine, ahead], [other]
    for step in range(2, places):
        first.append(pass_on(first[-1]))
    for step in range(1, places):
        second.append([pass_on(x) for x in second[-1]])
    pieces = second[-1]

    out = jnp.zeros((part, blk * queries), f32)

    def put(out, total, step, at):
        origin = (place - step + places) % places
        return lax.dynamic_update_slice_in_dim(out, total, origin * (2 * queries) + at, 1)

    def over_cores(keep, give):
        got = swap_cores(give).astype(f32)
        return keep[:part] + got[:part], (keep[part:] + got[part:]).astype(bf16)

    besides = []
    last = ()
    for step in range(places - 2):
        keep, give = score(spot, own, far, [first[step]] + second[step], *last)
        total, reach = over_cores(keep, give)
        besides.append(swap_across(reach))
        out = put(out, total + besides[-1].astype(f32), step, 0)
        last = (give,)

    keep, give = score(spot, own, far, first[-2:], *last, besides[0])
    early, early_reach = over_cores(keep, give)
    early_beside = swap_across(early_reach)
    keep, give = score(spot, own, far, second[-2], give, *besides)
    late, late_reach = over_cores(keep, give)
    late_beside = swap_across(late_reach)
    out = put(out, early[:, :queries] + late_beside.astype(f32), places - 2, side * queries)
    out = put(out, late + early_beside[:, :queries].astype(f32), places - 2, (1 - side) * queries)

    size = queries // 2
    last = (give,)
    for i, piece in enumerate(pieces):
        near, give, facing, opposite = last_score(own, far, piece, *last)
        cut = slice(queries + i * size, queries + (i + 1) * size)
        mine_total = early[:, cut] + swap_across(facing).astype(f32) + swap_diagonal(opposite).astype(f32)
        other_total = near + swap_cores(give).astype(f32) + early_beside[:, cut].astype(f32)
        out = put(out, mine_total, places - 1, side * queries + i * size)
        out = put(out, other_total, places - 1, (1 - side) * queries + i * size)
        last = (near, late_reach)
    return out


def solution(mesh):
    placed = (
        P(("grp", "blk"), "proj", None, None),
        P(("grp", "blk"), "proj", None, None),
        P(("grp", "blk"), None),
        P(("grp", "blk"), "proj"),
    )
    return jax.shard_map(
        on_device,
        mesh=mesh,
        in_specs=placed,
        out_specs=P(("grp", "blk", "proj"), None),
        check_vma=False,
    )
```

```python
import functools

import jax
import jax.numpy as jnp
from jax import lax
from jax.experimental import pallas as pl
from jax.experimental.pallas import tpu as pltpu
from jax.sharding import PartitionSpec as P

LANES = 128
VMEM_LIMIT = 48 * 1024 * 1024
ANYWHERE = pl.BlockSpec(memory_space=pl.ANY)
SCALARS = pl.BlockSpec(memory_space=pltpu.SMEM)
WHOLE = pl.BlockSpec(memory_space=pltpu.VMEM)
NT = (((1,), (1,)), ((), ()))
bf16, f32 = jnp.bfloat16, jnp.float32
LIMIT = pltpu.CompilerParams(vmem_limit_bytes=VMEM_LIMIT)


def shaped(kind, *shape):
    return jax.ShapeDtypeStruct(shape, kind)


def prepare_body(spot, query_grads, mine, *sending):
    rank = LANES // 2
    rows, width = query_grads.shape
    for outs, side in (((mine,), spot[0]), (sending, 1 - spot[0])):
        for m in range(width // 4 // LANES):
            at = pl.multiple_of(side * (width // 4) + m * LANES, LANES)
            low = query_grads[:, pl.ds(at, LANES)]
            high = query_grads[:, pl.ds(at + width // 2, LANES)]
            even = jnp.concatenate([low[:, :rank], high[:, :rank]], 1)
            odd = jnp.concatenate([low[:, rank:], high[:, rank:]], 1)
            for i, out in enumerate(outs):
                cut = slice(i * out.shape[0], (i + 1) * out.shape[0])
                out[:, 2 * m * LANES:(2 * m + 1) * LANES] = even[cut, :]
                out[:, (2 * m + 1) * LANES:(2 * m + 2) * LANES] = odd[cut, :]


def prepare(query_grads, spot):
    rows, width = query_grads.shape
    return pl.pallas_call(
        prepare_body,
        in_specs=[SCALARS, WHOLE],
        out_specs=[WHOLE] * 3,
        out_shape=[shaped(bf16, size, width // 2) for size in (rows, rows // 2, rows // 2)],
        compiler_params=LIMIT,
    )(spot, query_grads)


def form_body(rows, rank, spot, inputs, outgrads, mask, kept, sent, rounds):
    for d in range(rows):
        masked = outgrads[d] * mask[d:d + 1, :].astype(bf16)
        product = lax.dot_general(inputs[d], masked, NT, preferred_element_type=f32)
        pairs = jnp.concatenate([product[:rank // 2], product[rank // 2:]], 1)
        rounds[pl.ds(d, rank // 2, stride=rows), :] = pairs
    for out, side in ((kept, spot[0]), (sent, 1 - spot[0])):
        for k in range(rank // 4):
            at = pl.multiple_of((side * (rank // 4) + k) * rows, rows)
            out[:, k * LANES:(k + 1) * LANES] = rounds[pl.ds(at, rows), :].astype(bf16)


def form(doc_inputs, doc_outgrads, token_mask, spot):
    docs, rank, length = doc_inputs.shape
    rows = 64
    steps = docs // rows
    half = rank * rank // 2

    def at(g, spot):
        return lax.rem(g + spot[1] * (steps // 2), steps)

    return pl.pallas_call(
        functools.partial(form_body, rows, rank),
        grid_spec=pltpu.PrefetchScalarGridSpec(
            num_scalar_prefetch=1,
            grid=(steps,),
            in_specs=[
                pl.BlockSpec((rows, rank, length), lambda g, spot: (at(g, spot), 0, 0)),
                pl.BlockSpec((rows, rank, length), lambda g, spot: (at(g, spot), 0, 0)),
                pl.BlockSpec((rows, length), lambda g, spot: (at(g, spot), 0)),
            ],
            out_specs=[pl.BlockSpec((rows, half), lambda g, spot: (g, 0))] * 2,
            scratch_shapes=[pltpu.VMEM((rank // 2 * rows, LANES), f32)],
        ),
        out_shape=[shaped(bf16, docs, half)] * 2,
        compiler_params=LIMIT,
        cost_estimate=pl.CostEstimate(
            flops=40 * docs * rank * rank * length, bytes_accessed=4 * docs * rank * length + 2 * docs * rank * rank, transcendentals=0
        ),
    )(spot, doc_inputs, doc_outgrads, token_mask)


def tie(arrays, *after):
    count = len(arrays)
    return pl.pallas_call(
        lambda *refs: None,
        in_specs=[ANYWHERE] * (count + len(after)),
        out_specs=[ANYWHERE] * count,
        out_shape=[shaped(a.dtype, *a.shape) for a in arrays],
        input_output_aliases={i: i for i in range(count)},
        compiler_params=LIMIT,
    )(*arrays, *after)


def dot(rows, block):
    return lax.dot_general(rows, block, NT, preferred_element_type=f32)


FREE = pl.CostEstimate(flops=1024, bytes_accessed=1024, transcendentals=0)


def score_body(count, spot, own, far, *refs):
    keep, give = refs[-2:]
    part = own.shape[0] // 2
    for i, block in enumerate(refs[:count]):
        size = block.shape[0]
        if count == 3:
            rows = refs[0].shape[0]
            at = spot[0] * rows if i == 0 else (1 - spot[0]) * rows + (i - 1) * size
            columns = pl.ds(pl.multiple_of(at, size), size)
        else:
            columns = pl.ds(i * size, size)
        keep[:part, columns] = dot(own[:part, :], block[...])
        keep[part:, columns] = dot(far[:part, :], block[...])
        give[:part, columns] = dot(own[part:, :], block[...]).astype(bf16)
        give[part:, columns] = dot(far[part:, :], block[...]).astype(bf16)


def score(spot, own, far, blocks, *after):
    docs = own.shape[0]
    count = len(blocks)
    queries = sum(block.shape[0] for block in blocks)
    return pl.pallas_call(
        functools.partial(score_body, count),
        in_specs=[SCALARS] + [WHOLE] * (2 + count) + [ANYWHERE] * len(after),
        out_specs=[WHOLE] * 2,
        out_shape=[shaped(f32, docs, queries), shaped(bf16, docs, queries)],
        compiler_params=LIMIT,
        cost_estimate=FREE,
    )(spot, own, far, *blocks, *after)


def last_body(own, far, block, *refs):
    near, mate, across, diagonal = refs[-4:]
    part = near.shape[0]
    mate[...] = dot(own[part:, :], block[...]).astype(bf16)
    across[...] = dot(far[:part, :], block[...]).astype(bf16)
    diagonal[...] = dot(far[part:, :], block[...]).astype(bf16)
    near[...] = dot(own[:part, :], block[...])


def last_score(own, far, block, *after):
    shape = (own.shape[0] // 2, block.shape[0])
    return pl.pallas_call(
        last_body,
        in_specs=[WHOLE] * 3 + [ANYWHERE] * len(after),
        out_specs=[WHOLE] * 4,
        out_shape=[shaped(f32, *shape)] + [shaped(bf16, *shape)] * 3,
        compiler_params=LIMIT,
        cost_estimate=FREE,
    )(own, far, block, *after)


def on_device(doc_inputs, doc_outgrads, token_mask, query_grads):
    blk = lax.axis_size("blk")
    places = blk // 2
    me = lax.axis_index("blk")
    place, side = me // 2, me % 2
    spot = jnp.stack([side, lax.axis_index("proj")]).astype(jnp.int32)
    docs = doc_inputs.shape[0]
    queries = query_grads.shape[0]
    part = docs // 2

    across = [(b, b ^ 1) for b in range(blk)]
    onward = [(b, (b + 2) % blk) for b in range(blk)]
    diagonal = [(2 * b + c, 2 * (b ^ 1) + (c ^ 1)) for b in range(blk) for c in range(2)]

    def swap_across(x):
        return lax.ppermute(x, "blk", across)

    def swap_cores(x):
        return lax.ppermute(x, "proj", [(0, 1), (1, 0)])

    def pass_on(x):
        return lax.ppermute(x, "blk", onward)

    def swap_diagonal(x):
        return lax.ppermute(x, ("blk", "proj"), diagonal)

    mine, *sending = prepare(query_grads, spot)
    ahead = pass_on(mine)
    other = [swap_across(x) for x in sending]
    own, sent = form(
        doc_inputs.reshape(docs, *doc_inputs.shape[2:]), doc_outgrads.reshape(docs, *doc_outgrads.shape[2:]), token_mask, spot
    )
    sent, ahead, *other = tie((sent, ahead, *other))
    far = swap_across(sent)
    first, second = [mine, ahead], [other]
    for step in range(2, places):
        first.append(pass_on(first[-1]))
    for step in range(1, places):
        second.append([pass_on(x) for x in second[-1]])
    pieces = second[-1]

    out = jnp.zeros((part, blk * queries), f32)

    def put(out, total, step, at):
        origin = (place - step + places) % places
        return lax.dynamic_update_slice_in_dim(out, total, origin * (2 * queries) + at, 1)

    def over_cores(keep, give):
        got = swap_cores(give).astype(f32)
        return keep[:part] + got[:part], (keep[part:] + got[part:]).astype(bf16)

    besides = []
    last = ()
    for step in range(places - 2):
        keep, give = score(spot, own, far, [first[step]] + second[step], *last)
        total, reach = over_cores(keep, give)
        besides.append(swap_across(reach))
        out = put(out, total + besides[-1].astype(f32), step, 0)
        last = (give,)

    keep, give = score(spot, own, far, first[-2:], *last, besides[0], reach)
    early, early_reach = over_cores(keep, give)
    early_beside = swap_across(early_reach)
    keep, give = score(spot, own, far, second[-2], give)
    late, late_reach = over_cores(keep, give)
    late_beside = swap_across(late_reach)
    out = put(out, early[:, :queries] + late_beside.astype(f32), places - 2, side * queries)
    out = put(out, late + early_beside[:, :queries].astype(f32), places - 2, (1 - side) * queries)

    size = queries // 2
    last = (give, early_reach)
    for i, piece in enumerate(pieces):
        near, give, facing, opposite = last_score(own, far, piece, *last)
        cut = slice(queries + i * size, queries + (i + 1) * size)
        faced, opposed = swap_across(facing), swap_diagonal(opposite)
        mine_total = early[:, cut] + faced.astype(f32) + opposed.astype(f32)
        other_total = near + swap_cores(give).astype(f32) + early_beside[:, cut].astype(f32)
        out = put(out, mine_total, places - 1, side * queries + i * size)
        out = put(out, other_total, places - 1, (1 - side) * queries + i * size)
        last = (near, faced, opposed)
    return out


def solution(mesh):
    placed = (
        P(("grp", "blk"), "proj", None, None),
        P(("grp", "blk"), "proj", None, None),
        P(("grp", "blk"), None),
        P(("grp", "blk"), "proj"),
    )
    return jax.shard_map(
        on_device,
        mesh=mesh,
        in_specs=placed,
        out_specs=P(("grp", "blk", "proj"), None),
        check_vma=False,
    )
```

```python
import functools

import jax
import jax.numpy as jnp
from jax import lax
from jax.experimental import pallas as pl
from jax.experimental.pallas import tpu as pltpu
from jax.sharding import PartitionSpec as P

LANES = 128
VMEM_LIMIT = 48 * 1024 * 1024
ANYWHERE = pl.BlockSpec(memory_space=pl.ANY)
SCALARS = pl.BlockSpec(memory_space=pltpu.SMEM)
WHOLE = pl.BlockSpec(memory_space=pltpu.VMEM)
NT = (((1,), (1,)), ((), ()))
bf16, f32 = jnp.bfloat16, jnp.float32
LIMIT = pltpu.CompilerParams(vmem_limit_bytes=VMEM_LIMIT)


def shaped(kind, *shape):
    return jax.ShapeDtypeStruct(shape, kind)


def prepare_body(spot, query_grads, mine, *sending):
    rank = LANES // 2
    rows, width = query_grads.shape
    for outs, side in (((mine,), spot[0]), (sending, 1 - spot[0])):
        for m in range(width // 4 // LANES):
            at = pl.multiple_of(side * (width // 4) + m * LANES, LANES)
            low = query_grads[:, pl.ds(at, LANES)]
            high = query_grads[:, pl.ds(at + width // 2, LANES)]
            even = jnp.concatenate([low[:, :rank], high[:, :rank]], 1)
            odd = jnp.concatenate([low[:, rank:], high[:, rank:]], 1)
            for i, out in enumerate(outs):
                cut = slice(i * out.shape[0], (i + 1) * out.shape[0])
                out[:, 2 * m * LANES:(2 * m + 1) * LANES] = even[cut, :]
                out[:, (2 * m + 1) * LANES:(2 * m + 2) * LANES] = odd[cut, :]


def prepare(query_grads, spot):
    rows, width = query_grads.shape
    return pl.pallas_call(
        prepare_body,
        in_specs=[SCALARS, WHOLE],
        out_specs=[WHOLE] * 3,
        out_shape=[shaped(bf16, size, width // 2) for size in (rows, rows // 2, rows // 2)],
        compiler_params=pltpu.CompilerParams(vmem_limit_bytes=60 * 1024 * 1024),
    )(spot, query_grads)


def form_body(rows, rank, spot, inputs, outgrads, mask, kept, sent, rounds):
    for d in range(rows):
        masked = outgrads[d] * mask[d:d + 1, :].astype(bf16)
        product = lax.dot_general(inputs[d], masked, NT, preferred_element_type=f32)
        pairs = jnp.concatenate([product[:rank // 2], product[rank // 2:]], 1)
        rounds[pl.ds(d, rank // 2, stride=rows), :] = pairs
    for out, side in ((kept, spot[0]), (sent, 1 - spot[0])):
        for k in range(rank // 4):
            at = pl.multiple_of((side * (rank // 4) + k) * rows, rows)
            out[:, k * LANES:(k + 1) * LANES] = rounds[pl.ds(at, rows), :].astype(bf16)


def form(doc_inputs, doc_outgrads, token_mask, spot):
    docs, rank, length = doc_inputs.shape
    rows = 64
    steps = docs // rows
    half = rank * rank // 2

    def at(g, spot):
        return lax.rem(g + spot[1] * (steps // 2), steps)

    return pl.pallas_call(
        functools.partial(form_body, rows, rank),
        grid_spec=pltpu.PrefetchScalarGridSpec(
            num_scalar_prefetch=1,
            grid=(steps,),
            in_specs=[
                pl.BlockSpec((rows, rank, length), lambda g, spot: (at(g, spot), 0, 0)),
                pl.BlockSpec((rows, rank, length), lambda g, spot: (at(g, spot), 0, 0)),
                pl.BlockSpec((rows, length), lambda g, spot: (at(g, spot), 0)),
            ],
            out_specs=[pl.BlockSpec((rows, half), lambda g, spot: (g, 0))] * 2,
            scratch_shapes=[pltpu.VMEM((rank // 2 * rows, LANES), f32)],
        ),
        out_shape=[shaped(bf16, docs, half)] * 2,
        compiler_params=LIMIT,
        cost_estimate=pl.CostEstimate(
            flops=40 * docs * rank * rank * length, bytes_accessed=4 * docs * rank * length + 2 * docs * rank * rank, transcendentals=0
        ),
    )(spot, doc_inputs, doc_outgrads, token_mask)


def tie(arrays, *after):
    count = len(arrays)
    return pl.pallas_call(
        lambda *refs: None,
        in_specs=[ANYWHERE] * (count + len(after)),
        out_specs=[ANYWHERE] * count,
        out_shape=[shaped(a.dtype, *a.shape) for a in arrays],
        input_output_aliases={i: i for i in range(count)},
        compiler_params=LIMIT,
    )(*arrays, *after)


def dot(rows, block):
    return lax.dot_general(rows, block, NT, preferred_element_type=f32)


FREE = pl.CostEstimate(flops=1024, bytes_accessed=1024, transcendentals=0)


def score_body(count, spot, own, far, *refs):
    keep, give = refs[-2:]
    part = own.shape[0] // 2
    for i, block in enumerate(refs[:count]):
        size = block.shape[0]
        if count == 3:
            rows = refs[0].shape[0]
            at = spot[0] * rows if i == 0 else (1 - spot[0]) * rows + (i - 1) * size
            columns = pl.ds(pl.multiple_of(at, size), size)
        else:
            columns = pl.ds(i * size, size)
        keep[:part, columns] = dot(own[:part, :], block[...])
        keep[part:, columns] = dot(far[:part, :], block[...])
        give[:part, columns] = dot(own[part:, :], block[...]).astype(bf16)
        give[part:, columns] = dot(far[part:, :], block[...]).astype(bf16)


def score(spot, own, far, blocks, *after):
    docs = own.shape[0]
    count = len(blocks)
    queries = sum(block.shape[0] for block in blocks)
    return pl.pallas_call(
        functools.partial(score_body, count),
        in_specs=[SCALARS] + [WHOLE] * (2 + count) + [ANYWHERE] * len(after),
        out_specs=[WHOLE] * 2,
        out_shape=[shaped(f32, docs, queries), shaped(bf16, docs, queries)],
        compiler_params=LIMIT,
        cost_estimate=FREE,
    )(spot, own, far, *blocks, *after)


def last_body(own, far, block, *refs):
    near, mate, across, diagonal = refs[-4:]
    part = near.shape[0]
    mate[...] = dot(own[part:, :], block[...]).astype(bf16)
    across[...] = dot(far[:part, :], block[...]).astype(bf16)
    diagonal[...] = dot(far[part:, :], block[...]).astype(bf16)
    near[...] = dot(own[:part, :], block[...])


def last_score(own, far, block, *after):
    shape = (own.shape[0] // 2, block.shape[0])
    return pl.pallas_call(
        last_body,
        in_specs=[WHOLE] * 3 + [ANYWHERE] * len(after),
        out_specs=[WHOLE] * 4,
        out_shape=[shaped(f32, *shape)] + [shaped(bf16, *shape)] * 3,
        compiler_params=LIMIT,
        cost_estimate=FREE,
    )(own, far, block, *after)


def on_device(doc_inputs, doc_outgrads, token_mask, query_grads):
    blk = lax.axis_size("blk")
    places = blk // 2
    me = lax.axis_index("blk")
    place, side = me // 2, me % 2
    spot = jnp.stack([side, lax.axis_index("proj")]).astype(jnp.int32)
    docs = doc_inputs.shape[0]
    queries = query_grads.shape[0]
    part = docs // 2

    across = [(b, b ^ 1) for b in range(blk)]
    onward = [(b, (b + 2) % blk) for b in range(blk)]
    diagonal = [(2 * b + c, 2 * (b ^ 1) + (c ^ 1)) for b in range(blk) for c in range(2)]

    def swap_across(x):
        return lax.ppermute(x, "blk", across)

    def swap_cores(x):
        return lax.ppermute(x, "proj", [(0, 1), (1, 0)])

    def pass_on(x):
        return lax.ppermute(x, "blk", onward)

    def swap_diagonal(x):
        return lax.ppermute(x, ("blk", "proj"), diagonal)

    mine, *sending = prepare(query_grads, spot)
    ahead = pass_on(mine)
    other = [swap_across(x) for x in sending]
    own, sent = form(
        doc_inputs.reshape(docs, *doc_inputs.shape[2:]), doc_outgrads.reshape(docs, *doc_outgrads.shape[2:]), token_mask, spot
    )
    sent, ahead, *other = tie((sent, ahead, *other))
    far = swap_across(sent)
    first, second = [mine, ahead], [other]
    for step in range(2, places):
        first.append(pass_on(first[-1]))
    for step in range(1, places):
        second.append([pass_on(x) for x in second[-1]])
    pieces = second[-1]

    out = jnp.zeros((part, blk * queries), f32)

    def put(out, total, step, at):
        origin = (place - step + places) % places
        return lax.dynamic_update_slice_in_dim(out, total, origin * (2 * queries) + at, 1)

    def over_cores(keep, give):
        got = swap_cores(give).astype(f32)
        return keep[:part] + got[:part], (keep[part:] + got[part:]).astype(bf16)

    besides = []
    last = ()
    for step in range(places - 2):
        keep, give = score(spot, own, far, [first[step]] + second[step], *last)
        total, reach = over_cores(keep, give)
        besides.append(swap_across(reach))
        out = put(out, total + besides[-1].astype(f32), step, 0)
        last = (give,)

    keep, give = score(spot, own, far, first[-2:], *last, besides[0], reach)
    early, early_reach = over_cores(keep, give)
    early_beside = swap_across(early_reach)
    keep, give = score(spot, own, far, second[-2], give)
    late, late_reach = over_cores(keep, give)
    late_beside = swap_across(late_reach)
    out = put(out, early[:, :queries] + late_beside.astype(f32), places - 2, side * queries)
    out = put(out, late + early_beside[:, :queries].astype(f32), places - 2, (1 - side) * queries)

    size = queries // 2
    last = (give, early_reach)
    for i, piece in enumerate(pieces):
        near, give, facing, opposite = last_score(own, far, piece, *last)
        cut = slice(queries + i * size, queries + (i + 1) * size)
        faced, opposed = swap_across(facing), swap_diagonal(opposite)
        mine_total = early[:, cut] + faced.astype(f32) + opposed.astype(f32)
        other_total = near + swap_cores(give).astype(f32) + early_beside[:, cut].astype(f32)
        out = put(out, other_total, places - 1, (1 - side) * queries + i * size)
        out = put(out, mine_total, places - 1, side * queries + i * size)
        last = (near, faced, opposed)
    return out


def solution(mesh):
    placed = (
        P(("grp", "blk"), "proj", None, None),
        P(("grp", "blk"), "proj", None, None),
        P(("grp", "blk"), None),
        P(("grp", "blk"), "proj"),
    )
    return jax.shard_map(
        on_device,
        mesh=mesh,
        in_specs=placed,
        out_specs=P(("grp", "blk", "proj"), None),
        check_vma=False,
    )
```

```python
import functools

import jax
import jax.numpy as jnp
from jax import lax
from jax.experimental import pallas as pl
from jax.experimental.pallas import tpu as pltpu
from jax.sharding import PartitionSpec as P

LANES = 128
VMEM_LIMIT = 48 * 1024 * 1024
ANYWHERE = pl.BlockSpec(memory_space=pl.ANY)
SCALARS = pl.BlockSpec(memory_space=pltpu.SMEM)
WHOLE = pl.BlockSpec(memory_space=pltpu.VMEM)
NT = (((1,), (1,)), ((), ()))
bf16, f32 = jnp.bfloat16, jnp.float32
LIMIT = pltpu.CompilerParams(vmem_limit_bytes=VMEM_LIMIT)


def shaped(kind, *shape):
    return jax.ShapeDtypeStruct(shape, kind)


def prepare_body(spot, query_grads, mine, *sending):
    rank = LANES // 2
    rows, width = query_grads.shape
    for outs, side in (((mine,), spot[0]), (sending, 1 - spot[0])):
        for m in range(width // 4 // LANES):
            at = pl.multiple_of(side * (width // 4) + m * LANES, LANES)
            low = query_grads[:, pl.ds(at, LANES)]
            high = query_grads[:, pl.ds(at + width // 2, LANES)]
            even = jnp.concatenate([low[:, :rank], high[:, :rank]], 1)
            odd = jnp.concatenate([low[:, rank:], high[:, rank:]], 1)
            for i, out in enumerate(outs):
                cut = slice(i * out.shape[0], (i + 1) * out.shape[0])
                out[:, 2 * m * LANES:(2 * m + 1) * LANES] = even[cut, :]
                out[:, (2 * m + 1) * LANES:(2 * m + 2) * LANES] = odd[cut, :]


def prepare(query_grads, spot):
    rows, width = query_grads.shape
    return pl.pallas_call(
        prepare_body,
        in_specs=[SCALARS, WHOLE],
        out_specs=[WHOLE] * 3,
        out_shape=[shaped(bf16, size, width // 2) for size in (rows, rows // 2, rows // 2)],
        compiler_params=LIMIT,
    )(spot, query_grads)


def form_body(rows, rank, spot, inputs, outgrads, mask, kept, sent, rounds):
    for d in range(rows):
        masked = outgrads[d] * mask[d:d + 1, :].astype(bf16)
        product = lax.dot_general(inputs[d], masked, NT, preferred_element_type=f32)
        pairs = jnp.concatenate([product[:rank // 2], product[rank // 2:]], 1)
        rounds[pl.ds(d, rank // 2, stride=rows), :] = pairs
    for out, side in ((kept, spot[0]), (sent, 1 - spot[0])):
        for k in range(rank // 4):
            at = pl.multiple_of((side * (rank // 4) + k) * rows, rows)
            out[:, k * LANES:(k + 1) * LANES] = rounds[pl.ds(at, rows), :].astype(bf16)


def form(doc_inputs, doc_outgrads, token_mask, spot):
    docs, rank, length = doc_inputs.shape
    rows = 64
    steps = docs // rows
    half = rank * rank // 2

    def at(g, spot):
        return lax.rem(g + spot[1] * (steps // 2), steps)

    return pl.pallas_call(
        functools.partial(form_body, rows, rank),
        grid_spec=pltpu.PrefetchScalarGridSpec(
            num_scalar_prefetch=1,
            grid=(steps,),
            in_specs=[
                pl.BlockSpec((rows, rank, length), lambda g, spot: (at(g, spot), 0, 0)),
                pl.BlockSpec((rows, rank, length), lambda g, spot: (at(g, spot), 0, 0)),
                pl.BlockSpec((rows, length), lambda g, spot: (at(g, spot), 0)),
            ],
            out_specs=[pl.BlockSpec((rows, half), lambda g, spot: (g, 0))] * 2,
            scratch_shapes=[pltpu.VMEM((rank // 2 * rows, LANES), f32)],
        ),
        out_shape=[shaped(bf16, docs, half)] * 2,
        compiler_params=LIMIT,
        cost_estimate=pl.CostEstimate(
            flops=40 * docs * rank * rank * length, bytes_accessed=4 * docs * rank * length + 2 * docs * rank * rank, transcendentals=0
        ),
    )(spot, doc_inputs, doc_outgrads, token_mask)


def tie(arrays, *after):
    count = len(arrays)
    return pl.pallas_call(
        lambda *refs: None,
        in_specs=[ANYWHERE] * (count + len(after)),
        out_specs=[ANYWHERE] * count,
        out_shape=[shaped(a.dtype, *a.shape) for a in arrays],
        input_output_aliases={i: i for i in range(count)},
        compiler_params=LIMIT,
    )(*arrays, *after)


def dot(rows, block):
    return lax.dot_general(rows, block, NT, preferred_element_type=f32)


FREE = pl.CostEstimate(flops=1024, bytes_accessed=1024, transcendentals=0)


def score_body(count, spot, own, far, *refs):
    keep, give = refs[-2:]
    part = own.shape[0] // 2
    for i, block in enumerate(refs[:count]):
        size = block.shape[0]
        if count == 3:
            rows = refs[0].shape[0]
            at = spot[0] * rows if i == 0 else (1 - spot[0]) * rows + (i - 1) * size
            columns = pl.ds(pl.multiple_of(at, size), size)
        else:
            columns = pl.ds(i * size, size)
        keep[:part, columns] = dot(own[:part, :], block[...])
        keep[part:, columns] = dot(far[:part, :], block[...])
        give[:part, columns] = dot(own[part:, :], block[...]).astype(bf16)
        give[part:, columns] = dot(far[part:, :], block[...]).astype(bf16)


def score(spot, own, far, blocks, *after):
    docs = own.shape[0]
    count = len(blocks)
    queries = sum(block.shape[0] for block in blocks)
    return pl.pallas_call(
        functools.partial(score_body, count),
        in_specs=[SCALARS] + [WHOLE] * (2 + count) + [ANYWHERE] * len(after),
        out_specs=[WHOLE] * 2,
        out_shape=[shaped(f32, docs, queries), shaped(bf16, docs, queries)],
        compiler_params=LIMIT,
        cost_estimate=FREE,
    )(spot, own, far, *blocks, *after)


def last_body(own, far, block, *refs):
    near, mate, across, diagonal = refs[-4:]
    part = near.shape[0]
    mate[...] = dot(own[part:, :], block[...]).astype(bf16)
    across[...] = dot(far[:part, :], block[...]).astype(bf16)
    diagonal[...] = dot(far[part:, :], block[...]).astype(bf16)
    near[...] = dot(own[:part, :], block[...])


def last_score(own, far, block, *after):
    shape = (own.shape[0] // 2, block.shape[0])
    return pl.pallas_call(
        last_body,
        in_specs=[WHOLE] * 3 + [ANYWHERE] * len(after),
        out_specs=[WHOLE] * 4,
        out_shape=[shaped(f32, *shape)] + [shaped(bf16, *shape)] * 3,
        compiler_params=LIMIT,
        cost_estimate=FREE,
    )(own, far, block, *after)


def on_device(doc_inputs, doc_outgrads, token_mask, query_grads):
    blk = lax.axis_size("blk")
    places = blk // 2
    me = lax.axis_index("blk")
    place, side = me // 2, me % 2
    spot = jnp.stack([side, lax.axis_index("proj")]).astype(jnp.int32)
    docs = doc_inputs.shape[0]
    queries = query_grads.shape[0]
    part = docs // 2

    across = [(b, b ^ 1) for b in range(blk)]
    onward = [(b, (b + 2) % blk) for b in range(blk)]
    diagonal = [(2 * b + c, 2 * (b ^ 1) + (c ^ 1)) for b in range(blk) for c in range(2)]

    def swap_across(x):
        return lax.ppermute(x, "blk", across)

    def swap_cores(x):
        return lax.ppermute(x, "proj", [(0, 1), (1, 0)])

    def pass_on(x):
        return lax.ppermute(x, "blk", onward)

    def swap_diagonal(x):
        return lax.ppermute(x, ("blk", "proj"), diagonal)

    mine, *sending = prepare(query_grads, spot)
    ahead = pass_on(mine)
    other = [swap_across(x) for x in sending]
    own, sent = form(
        doc_inputs.reshape(docs, *doc_inputs.shape[2:]), doc_outgrads.reshape(docs, *doc_outgrads.shape[2:]), token_mask, spot
    )
    sent, ahead, *other = tie((sent, ahead, *other))
    far = swap_across(sent)
    first, second = [mine, ahead], [other]
    for step in range(2, places):
        first.append(pass_on(first[-1]))
    for step in range(1, places):
        second.append([pass_on(x) for x in second[-1]])
    pieces = second[-1]

    out = jnp.zeros((part, blk * queries), f32)

    def put(out, total, step, at):
        origin = (place - step + places) % places
        return lax.dynamic_update_slice_in_dim(out, total, origin * (2 * queries) + at, 1)

    def over_cores(keep, give):
        got = swap_cores(give).astype(f32)
        return keep[:part] + got[:part], (keep[part:] + got[part:]).astype(bf16)

    besides = []
    last = ()
    for step in range(places - 2):
        keep, give = score(spot, own, far, [first[step]] + second[step], *last)
        total, reach = over_cores(keep, give)
        besides.append(swap_across(reach))
        out = put(out, total + besides[-1].astype(f32), step, 0)
        last = (give,)

    keep, give = score(spot, own, far, first[-2:], *last, besides[0], reach)
    early, early_reach = over_cores(keep, give)
    early_beside = swap_across(early_reach)
    keep, give = score(spot, own, far, second[-2], give)
    late, late_reach = over_cores(keep, give)
    late_beside = swap_across(late_reach)
    out = put(out, early[:, :queries] + late_beside.astype(f32), places - 2, side * queries)
    out = put(out, late + early_beside[:, :queries].astype(f32), places - 2, (1 - side) * queries)

    size = queries // 2
    last = (give, early_reach)
    for i, piece in enumerate(pieces):
        near, give, facing, opposite = last_score(own, far, piece, *last)
        cut = slice(queries + i * size, queries + (i + 1) * size)
        faced, opposed = swap_across(facing), swap_diagonal(opposite)
        mine_total = early[:, cut] + faced.astype(f32) + opposed.astype(f32)
        other_total = near + swap_cores(give).astype(f32) + early_beside[:, cut].astype(f32)
        out = put(out, other_total, places - 1, (1 - side) * queries + i * size)
        out = put(out, mine_total, places - 1, side * queries + i * size)
        last = (near, faced, opposed)
    return out


def solution(mesh):
    placed = (
        P(("grp", "blk"), "proj", None, None),
        P(("grp", "blk"), "proj", None, None),
        P(("grp", "blk"), None),
        P(("grp", "blk"), "proj"),
    )
    return jax.shard_map(
        on_device,
        mesh=mesh,
        in_specs=placed,
        out_specs=P(("grp", "blk", "proj"), None),
        check_vma=False,
    )
```

```python
import functools

import jax
import jax.numpy as jnp
from jax import lax
from jax.experimental import pallas as pl
from jax.experimental.pallas import tpu as pltpu
from jax.sharding import PartitionSpec as P

LANES = 128
VMEM_LIMIT = 48 * 1024 * 1024
ANYWHERE = pl.BlockSpec(memory_space=pl.ANY)
SCALARS = pl.BlockSpec(memory_space=pltpu.SMEM)
WHOLE = pl.BlockSpec(memory_space=pltpu.VMEM)
NT = (((1,), (1,)), ((), ()))
bf16, f32 = jnp.bfloat16, jnp.float32
LIMIT = pltpu.CompilerParams(vmem_limit_bytes=VMEM_LIMIT)


def shaped(kind, *shape):
    return jax.ShapeDtypeStruct(shape, kind)


def prepare_body(spot, query_grads, mine, *sending):
    rank = LANES // 2
    rows, width = query_grads.shape
    for outs, side in (((mine,), spot[0]), (sending, 1 - spot[0])):
        for m in range(width // 4 // LANES):
            at = pl.multiple_of(side * (width // 4) + m * LANES, LANES)
            low = query_grads[:, pl.ds(at, LANES)]
            high = query_grads[:, pl.ds(at + width // 2, LANES)]
            even = jnp.concatenate([low[:, :rank], high[:, :rank]], 1)
            odd = jnp.concatenate([low[:, rank:], high[:, rank:]], 1)
            for i, out in enumerate(outs):
                cut = slice(i * out.shape[0], (i + 1) * out.shape[0])
                out[:, 2 * m * LANES:(2 * m + 1) * LANES] = even[cut, :]
                out[:, (2 * m + 1) * LANES:(2 * m + 2) * LANES] = odd[cut, :]


def prepare(query_grads, spot):
    rows, width = query_grads.shape
    return pl.pallas_call(
        prepare_body,
        in_specs=[SCALARS, WHOLE],
        out_specs=[WHOLE] * 3,
        out_shape=[shaped(bf16, size, width // 2) for size in (rows, rows // 2, rows // 2)],
        compiler_params=LIMIT,
    )(spot, query_grads)


def form_body(rows, rank, spot, inputs, outgrads, mask, kept, sent, sent_rest, rounds):
    for d in range(rows):
        masked = outgrads[d] * mask[d:d + 1, :].astype(bf16)
        product = lax.dot_general(inputs[d], masked, NT, preferred_element_type=f32)
        pairs = jnp.concatenate([product[:rank // 2], product[rank // 2:]], 1)
        rounds[pl.ds(d, rank // 2, stride=rows), :] = pairs
    for side, outs in ((spot[0], (kept,)), (1 - spot[0], (sent, sent_rest))):
        for k in range(rank // 4):
            at = pl.multiple_of((side * (rank // 4) + k) * rows, rows)
            out, place = outs[k * len(outs) // (rank // 4)], k % (rank // 4 // len(outs))
            out[:, place * LANES:(place + 1) * LANES] = rounds[pl.ds(at, rows), :].astype(bf16)


def form(doc_inputs, doc_outgrads, token_mask, spot):
    docs, rank, length = doc_inputs.shape
    rows = 64
    steps = docs // rows
    half = rank * rank // 2
    widths = (half, half // 2, half // 2)

    def at(g, spot):
        return lax.rem(g + spot[1] * (steps // 2), steps)

    return pl.pallas_call(
        functools.partial(form_body, rows, rank),
        grid_spec=pltpu.PrefetchScalarGridSpec(
            num_scalar_prefetch=1,
            grid=(steps,),
            in_specs=[
                pl.BlockSpec((rows, rank, length), lambda g, spot: (at(g, spot), 0, 0)),
                pl.BlockSpec((rows, rank, length), lambda g, spot: (at(g, spot), 0, 0)),
                pl.BlockSpec((rows, length), lambda g, spot: (at(g, spot), 0)),
            ],
            out_specs=[pl.BlockSpec((rows, width), lambda g, spot: (g, 0)) for width in widths],
            scratch_shapes=[pltpu.VMEM((rank // 2 * rows, LANES), f32)],
        ),
        out_shape=[shaped(bf16, docs, width) for width in widths],
        compiler_params=LIMIT,
        cost_estimate=pl.CostEstimate(
            flops=40 * docs * rank * rank * length, bytes_accessed=4 * docs * rank * length + 2 * docs * rank * rank, transcendentals=0
        ),
    )(spot, doc_inputs, doc_outgrads, token_mask)


def tie(arrays, *after):
    count = len(arrays)
    return pl.pallas_call(
        lambda *refs: None,
        in_specs=[ANYWHERE] * (count + len(after)),
        out_specs=[ANYWHERE] * count,
        out_shape=[shaped(a.dtype, *a.shape) for a in arrays],
        input_output_aliases={i: i for i in range(count)},
        compiler_params=LIMIT,
    )(*arrays, *after)


def dot(rows, block):
    return lax.dot_general(rows, block, NT, preferred_element_type=f32)


FREE = pl.CostEstimate(flops=1024, bytes_accessed=1024, transcendentals=0)


def reach(far, rest, rows, block):
    half = far.shape[1]
    return dot(far[rows, :], block[:, :half]) + dot(rest[rows, :], block[:, half:])


def score_body(count, spot, own, far, rest, *refs):
    keep, give = refs[-2:]
    part = own.shape[0] // 2
    for i, block in enumerate(refs[:count]):
        size = block.shape[0]
        if count == 3:
            rows = refs[0].shape[0]
            at = spot[0] * rows if i == 0 else (1 - spot[0]) * rows + (i - 1) * size
            columns = pl.ds(pl.multiple_of(at, size), size)
        else:
            columns = pl.ds(i * size, size)
        keep[:part, columns] = dot(own[:part, :], block[...])
        keep[part:, columns] = reach(far, rest, slice(part), block)
        give[:part, columns] = dot(own[part:, :], block[...]).astype(bf16)
        give[part:, columns] = reach(far, rest, slice(part, None), block).astype(bf16)


def score(spot, own, far, blocks, *after):
    docs = own.shape[0]
    count = len(blocks)
    queries = sum(block.shape[0] for block in blocks)
    return pl.pallas_call(
        functools.partial(score_body, count),
        in_specs=[SCALARS] + [WHOLE] * (3 + count) + [ANYWHERE] * len(after),
        out_specs=[WHOLE] * 2,
        out_shape=[shaped(f32, docs, queries), shaped(bf16, docs, queries)],
        compiler_params=LIMIT,
        cost_estimate=FREE,
    )(spot, own, *far, *blocks, *after)


def last_body(own, far, rest, block, *refs):
    near, mate, across, diagonal = refs[-4:]
    part = near.shape[0]
    mate[...] = dot(own[part:, :], block[...]).astype(bf16)
    across[...] = reach(far, rest, slice(part), block).astype(bf16)
    diagonal[...] = reach(far, rest, slice(part, None), block).astype(bf16)
    near[...] = dot(own[:part, :], block[...])


def last_score(own, far, block, *after):
    shape = (own.shape[0] // 2, block.shape[0])
    return pl.pallas_call(
        last_body,
        in_specs=[WHOLE] * 4 + [ANYWHERE] * len(after),
        out_specs=[WHOLE] * 4,
        out_shape=[shaped(f32, *shape)] + [shaped(bf16, *shape)] * 3,
        compiler_params=LIMIT,
        cost_estimate=FREE,
    )(own, *far, block, *after)


def on_device(doc_inputs, doc_outgrads, token_mask, query_grads):
    blk = lax.axis_size("blk")
    places = blk // 2
    me = lax.axis_index("blk")
    place, side = me // 2, me % 2
    spot = jnp.stack([side, lax.axis_index("proj")]).astype(jnp.int32)
    docs = doc_inputs.shape[0]
    queries = query_grads.shape[0]
    part = docs // 2

    across = [(b, b ^ 1) for b in range(blk)]
    onward = [(b, (b + 2) % blk) for b in range(blk)]
    diagonal = [(2 * b + c, 2 * (b ^ 1) + (c ^ 1)) for b in range(blk) for c in range(2)]

    def swap_across(x):
        return lax.ppermute(x, "blk", across)

    def swap_cores(x):
        return lax.ppermute(x, "proj", [(0, 1), (1, 0)])

    def pass_on(x):
        return lax.ppermute(x, "blk", onward)

    def swap_diagonal(x):
        return lax.ppermute(x, ("blk", "proj"), diagonal)

    mine, *sending = prepare(query_grads, spot)
    ahead = pass_on(mine)
    other = [swap_across(x) for x in sending]
    own, *sent = form(
        doc_inputs.reshape(docs, *doc_inputs.shape[2:]), doc_outgrads.reshape(docs, *doc_outgrads.shape[2:]), token_mask, spot
    )
    *sent, ahead, second_half, first_half = tie((*sent, ahead, *other[::-1]))
    other = [first_half, second_half]
    far = [swap_across(x) for x in sent]
    first, second = [mine, ahead], [other]
    for step in range(2, places):
        first.append(pass_on(first[-1]))
    for step in range(1, places):
        second.append([pass_on(x) for x in second[-1]])
    pieces = second[-1]

    out = jnp.zeros((part, blk * queries), f32)

    def put(out, total, step, at):
        origin = (place - step + places) % places
        return lax.dynamic_update_slice_in_dim(out, total, origin * (2 * queries) + at, 1)

    def over_cores(keep, give):
        got = swap_cores(give).astype(f32)
        return keep[:part] + got[:part], (keep[part:] + got[part:]).astype(bf16)

    besides = []
    last = ()
    for step in range(places - 2):
        keep, give = score(spot, own, far, [first[step]] + second[step], *last)
        total, reach = over_cores(keep, give)
        besides.append(swap_across(reach))
        out = put(out, total + besides[-1].astype(f32), step, 0)
        last = (give,)

    keep, give = score(spot, own, far, first[-2:], *last, besides[0], reach)
    early, early_reach = over_cores(keep, give)
    early_beside = swap_across(early_reach)
    keep, give = score(spot, own, far, second[-2], give)
    late, late_reach = over_cores(keep, give)
    late_beside = swap_across(late_reach)
    out = put(out, early[:, :queries] + late_beside.astype(f32), places - 2, side * queries)
    out = put(out, late + early_beside[:, :queries].astype(f32), places - 2, (1 - side) * queries)

    size = queries // 2
    last = (give, early_reach)
    for i, piece in enumerate(pieces):
        near, give, facing, opposite = last_score(own, far, piece, *last)
        cut = slice(queries + i * size, queries + (i + 1) * size)
        faced, opposed = swap_across(facing), swap_diagonal(opposite)
        mine_total = early[:, cut] + faced.astype(f32) + opposed.astype(f32)
        other_total = near + swap_cores(give).astype(f32) + early_beside[:, cut].astype(f32)
        out = put(out, other_total, places - 1, (1 - side) * queries + i * size)
        out = put(out, mine_total, places - 1, side * queries + i * size)
        last = (near, faced, opposed)
    return out


def solution(mesh):
    placed = (
        P(("grp", "blk"), "proj", None, None),
        P(("grp", "blk"), "proj", None, None),
        P(("grp", "blk"), None),
        P(("grp", "blk"), "proj"),
    )
    return jax.shard_map(
        on_device,
        mesh=mesh,
        in_specs=placed,
        out_specs=P(("grp", "blk", "proj"), None),
        check_vma=False,
    )
```

```python
import functools

import jax
import jax.numpy as jnp
from jax import lax
from jax.experimental import pallas as pl
from jax.experimental.pallas import tpu as pltpu
from jax.sharding import PartitionSpec as P

LANES = 128
VMEM_LIMIT = 48 * 1024 * 1024
ANYWHERE = pl.BlockSpec(memory_space=pl.ANY)
SCALARS = pl.BlockSpec(memory_space=pltpu.SMEM)
WHOLE = pl.BlockSpec(memory_space=pltpu.VMEM)
NT = (((1,), (1,)), ((), ()))
bf16, f32 = jnp.bfloat16, jnp.float32
LIMIT = pltpu.CompilerParams(vmem_limit_bytes=VMEM_LIMIT)


def shaped(kind, *shape):
    return jax.ShapeDtypeStruct(shape, kind)


def prepare_body(spot, query_grads, mine, first, second, low, high, sems):
    rank = LANES // 2
    rows, width = query_grads.shape
    quarter = width // 4
    copies = []
    for i in range(2):
        side = spot[0] if i == 0 else 1 - spot[0]
        for j, buffer in enumerate((low, high)):
            at = pl.ds(pl.multiple_of(side * quarter + j * (width // 2), LANES), quarter)
            copies.append(pltpu.make_async_copy(query_grads.at[:, at], buffer.at[i], sems.at[i, j]))
            copies[-1].start()
    for i, outs in enumerate(((mine,), (first, second))):
        copies[2 * i].wait()
        copies[2 * i + 1].wait()
        for m in range(quarter // LANES):
            at = slice(m * LANES, (m + 1) * LANES)
            lower, upper = low[i, :, at], high[i, :, at]
            even = jnp.concatenate([lower[:, :rank], upper[:, :rank]], 1)
            odd = jnp.concatenate([lower[:, rank:], upper[:, rank:]], 1)
            for n, out in enumerate(outs):
                cut = slice(n * out.shape[0], (n + 1) * out.shape[0])
                out[:, 2 * m * LANES:(2 * m + 1) * LANES] = even[cut, :]
                out[:, (2 * m + 1) * LANES:(2 * m + 2) * LANES] = odd[cut, :]


def prepare(query_grads, spot):
    rows, width = query_grads.shape
    return pl.pallas_call(
        prepare_body,
        in_specs=[SCALARS, ANYWHERE],
        out_specs=[WHOLE] * 3,
        out_shape=[shaped(bf16, size, width // 2) for size in (rows, rows // 2, rows // 2)],
        scratch_shapes=[pltpu.VMEM((2, rows, width // 4), bf16)] * 2 + [pltpu.SemaphoreType.DMA((2, 2))],
        compiler_params=pltpu.CompilerParams(vmem_limit_bytes=60 * 1024 * 1024),
    )(spot, query_grads)


def form_body(rows, rank, spot, inputs, outgrads, mask, kept, sent, sent_rest, rounds):
    for d in range(rows):
        masked = outgrads[d] * mask[d:d + 1, :].astype(bf16)
        product = lax.dot_general(inputs[d], masked, NT, preferred_element_type=f32)
        pairs = jnp.concatenate([product[:rank // 2], product[rank // 2:]], 1)
        rounds[pl.ds(d, rank // 2, stride=rows), :] = pairs
    for side, outs in ((spot[0], (kept,)), (1 - spot[0], (sent, sent_rest))):
        for k in range(rank // 4):
            at = pl.multiple_of((side * (rank // 4) + k) * rows, rows)
            out, place = outs[k * len(outs) // (rank // 4)], k % (rank // 4 // len(outs))
            out[:, place * LANES:(place + 1) * LANES] = rounds[pl.ds(at, rows), :].astype(bf16)


def form(doc_inputs, doc_outgrads, token_mask, spot):
    docs, rank, length = doc_inputs.shape
    rows = 64
    steps = docs // rows
    half = rank * rank // 2
    widths = (half, half // 2, half // 2)

    def at(g, spot):
        return lax.rem(g + spot[1] * (steps // 2), steps)

    return pl.pallas_call(
        functools.partial(form_body, rows, rank),
        grid_spec=pltpu.PrefetchScalarGridSpec(
            num_scalar_prefetch=1,
            grid=(steps,),
            in_specs=[
                pl.BlockSpec((rows, rank, length), lambda g, spot: (at(g, spot), 0, 0)),
                pl.BlockSpec((rows, rank, length), lambda g, spot: (at(g, spot), 0, 0)),
                pl.BlockSpec((rows, length), lambda g, spot: (at(g, spot), 0)),
            ],
            out_specs=[pl.BlockSpec((rows, width), lambda g, spot: (g, 0)) for width in widths],
            scratch_shapes=[pltpu.VMEM((rank // 2 * rows, LANES), f32)],
        ),
        out_shape=[shaped(bf16, docs, width) for width in widths],
        compiler_params=LIMIT,
        cost_estimate=pl.CostEstimate(
            flops=40 * docs * rank * rank * length, bytes_accessed=4 * docs * rank * length + 2 * docs * rank * rank, transcendentals=0
        ),
    )(spot, doc_inputs, doc_outgrads, token_mask)


def tie(arrays, *after):
    count = len(arrays)
    return pl.pallas_call(
        lambda *refs: None,
        in_specs=[ANYWHERE] * (count + len(after)),
        out_specs=[ANYWHERE] * count,
        out_shape=[shaped(a.dtype, *a.shape) for a in arrays],
        input_output_aliases={i: i for i in range(count)},
        compiler_params=LIMIT,
    )(*arrays, *after)


def dot(rows, block):
    return lax.dot_general(rows, block, NT, preferred_element_type=f32)


FREE = pl.CostEstimate(flops=1024, bytes_accessed=1024, transcendentals=0)


def reach(far, rest, rows, block):
    half = far.shape[1]
    return dot(far[rows, :], block[:, :half]) + dot(rest[rows, :], block[:, half:])


def score_body(count, spot, own, far, rest, *refs):
    keep, give = refs[-2:]
    part = own.shape[0] // 2
    for i, block in enumerate(refs[:count]):
        size = block.shape[0]
        if count == 3:
            rows = refs[0].shape[0]
            at = spot[0] * rows if i == 0 else (1 - spot[0]) * rows + (i - 1) * size
            columns = pl.ds(pl.multiple_of(at, size), size)
        else:
            columns = pl.ds(i * size, size)
        keep[:part, columns] = dot(own[:part, :], block[...])
        keep[part:, columns] = reach(far, rest, slice(part), block)
        give[:part, columns] = dot(own[part:, :], block[...]).astype(bf16)
        give[part:, columns] = reach(far, rest, slice(part, None), block).astype(bf16)


def score(spot, own, far, blocks, *after):
    docs = own.shape[0]
    count = len(blocks)
    queries = sum(block.shape[0] for block in blocks)
    return pl.pallas_call(
        functools.partial(score_body, count),
        in_specs=[SCALARS] + [WHOLE] * (3 + count) + [ANYWHERE] * len(after),
        out_specs=[WHOLE] * 2,
        out_shape=[shaped(f32, docs, queries), shaped(bf16, docs, queries)],
        compiler_params=LIMIT,
        cost_estimate=FREE,
    )(spot, own, *far, *blocks, *after)


def last_body(own, far, rest, block, *refs):
    near, mate, across, diagonal = refs[-4:]
    part = near.shape[0]
    mate[...] = dot(own[part:, :], block[...]).astype(bf16)
    across[...] = reach(far, rest, slice(part), block).astype(bf16)
    diagonal[...] = reach(far, rest, slice(part, None), block).astype(bf16)
    near[...] = dot(own[:part, :], block[...])


def last_score(own, far, block, *after):
    shape = (own.shape[0] // 2, block.shape[0])
    return pl.pallas_call(
        last_body,
        in_specs=[WHOLE] * 4 + [ANYWHERE] * len(after),
        out_specs=[WHOLE] * 4,
        out_shape=[shaped(f32, *shape)] + [shaped(bf16, *shape)] * 3,
        compiler_params=LIMIT,
        cost_estimate=FREE,
    )(own, *far, block, *after)


def on_device(doc_inputs, doc_outgrads, token_mask, query_grads):
    blk = lax.axis_size("blk")
    places = blk // 2
    me = lax.axis_index("blk")
    place, side = me // 2, me % 2
    spot = jnp.stack([side, lax.axis_index("proj")]).astype(jnp.int32)
    docs = doc_inputs.shape[0]
    queries = query_grads.shape[0]
    part = docs // 2

    across = [(b, b ^ 1) for b in range(blk)]
    onward = [(b, (b + 2) % blk) for b in range(blk)]
    diagonal = [(2 * b + c, 2 * (b ^ 1) + (c ^ 1)) for b in range(blk) for c in range(2)]

    def swap_across(x):
        return lax.ppermute(x, "blk", across)

    def swap_cores(x):
        return lax.ppermute(x, "proj", [(0, 1), (1, 0)])

    def pass_on(x):
        return lax.ppermute(x, "blk", onward)

    def swap_diagonal(x):
        return lax.ppermute(x, ("blk", "proj"), diagonal)

    mine, *sending = prepare(query_grads, spot)
    ahead = pass_on(mine)
    other = [swap_across(x) for x in sending]
    own, *sent = form(
        doc_inputs.reshape(docs, *doc_inputs.shape[2:]), doc_outgrads.reshape(docs, *doc_outgrads.shape[2:]), token_mask, spot
    )
    *sent, ahead, second_half, first_half = tie((*sent, ahead, *other[::-1]))
    other = [first_half, second_half]
    far = [swap_across(x) for x in sent]
    first, second = [mine, ahead], [other]
    for step in range(2, places):
        first.append(pass_on(first[-1]))
    for step in range(1, places):
        second.append([pass_on(x) for x in second[-1]])
    pieces = second[-1]

    out = jnp.zeros((part, blk * queries), f32)

    def put(out, total, step, at):
        origin = (place - step + places) % places
        return lax.dynamic_update_slice_in_dim(out, total, origin * (2 * queries) + at, 1)

    def over_cores(keep, give):
        got = swap_cores(give).astype(f32)
        return keep[:part] + got[:part], (keep[part:] + got[part:]).astype(bf16)

    besides = []
    last = ()
    for step in range(places - 2):
        keep, give = score(spot, own, far, [first[step]] + second[step], *last)
        total, reach = over_cores(keep, give)
        besides.append(swap_across(reach))
        out = put(out, total + besides[-1].astype(f32), step, 0)
        last = (give,)

    keep, give = score(spot, own, far, first[-2:], *last, besides[0], reach)
    early, early_reach = over_cores(keep, give)
    early_beside = swap_across(early_reach)
    keep, give = score(spot, own, far, second[-2], give)
    late, late_reach = over_cores(keep, give)
    late_beside = swap_across(late_reach)
    out = put(out, early[:, :queries] + late_beside.astype(f32), places - 2, side * queries)
    out = put(out, late + early_beside[:, :queries].astype(f32), places - 2, (1 - side) * queries)

    size = queries // 2
    last = (give, early_reach)
    for i, piece in enumerate(pieces):
        near, give, facing, opposite = last_score(own, far, piece, *last)
        cut = slice(queries + i * size, queries + (i + 1) * size)
        faced, opposed = swap_across(facing), swap_diagonal(opposite)
        mine_total = early[:, cut] + faced.astype(f32) + opposed.astype(f32)
        other_total = near + swap_cores(give).astype(f32) + early_beside[:, cut].astype(f32)
        out = put(out, other_total, places - 1, (1 - side) * queries + i * size)
        out = put(out, mine_total, places - 1, side * queries + i * size)
        last = (near, faced, opposed)
    return out


def solution(mesh):
    placed = (
        P(("grp", "blk"), "proj", None, None),
        P(("grp", "blk"), "proj", None, None),
        P(("grp", "blk"), None),
        P(("grp", "blk"), "proj"),
    )
    return jax.shard_map(
        on_device,
        mesh=mesh,
        in_specs=placed,
        out_specs=P(("grp", "blk", "proj"), None),
        check_vma=False,
    )
```
